32 devices in a mesh: row: 4 (over z), col: 8 (over y, x, core).
Axes of the slice: x: 2, y: 2, z: 4, core: 2. Of those that a mesh axis runs over, the one named last changes fastest.
Arguments:
- gate_pre: bfloat16 [1024, 16384], P('row', 'col'), may hold values from -8 to 8
- up_pre: bfloat16 [1024, 16384], P('row', 'col'), may hold values from -6 to 6
- down_t: bfloat16 [4096, 16384], P('row', 'col'), may hold values from -0.09375 to 0.09375
- grad_out: bfloat16 [1024, 4096], P('row', 'col'), may hold values from -6 to 6
Outputs:
- gate_grad: bfloat16 [1024, 16384], P('row', 'col')
- up_grad: bfloat16 [1024, 16384], P('row', 'col')
- weight_grad: bfloat16 [4096, 16384], P('row', 'col')
The draws below stay inside these ranges and needn't reach their ends.
All inputs are finite; a program needn't handle non-finite values.
Results may differ from the reference program's by a relative error of at most 0.0049.
Values may be sent and summed in bfloat16 or wider, within the bound.
No kernel may reach another device: no remote copies, remote signals or barrier semaphores. Data moves between devices by JAX's collectives and lax.ppermute only.
A program may use at most 128 MiB of HBM per device.

```python
import jax
import jax.numpy as jnp

D = 4096
FF = 16384
TOKENS = 1024


def raised(drawn, own_key, source, target, shards_of, factor):
    owner, partner = [(jnp.arange(drawn.shape[axis_at]) // (drawn.shape[axis_at] // shards_of)).reshape([-1 if axis == axis_at else 1 for axis in range(drawn.ndim)]) for axis_at in (source, target)]
    chosen = jax.random.permutation(own_key, shards_of)[partner]
    strong = (owner == chosen) | (owner == (partner + shards_of // 2) % shards_of)
    return jnp.where(strong, factor * drawn, drawn)


def block_scale(own_key, dims, pieces, least, largest):
    def one(dim, shards_of):
        heights = jax.random.uniform(jax.random.fold_in(jax.random.fold_in(own_key, 6), dim), (shards_of,), jnp.float32, least / len(pieces), largest / len(pieces))
        return jnp.repeat(jnp.exp(heights), dims[dim] // shards_of).reshape((-1,) + (1,) * (len(dims) - dim - 1))

    gain = one(*pieces[0])
    for cut in pieces[1:]:
        gain = gain * one(*cut)
    return gain


def normal_values(stream_key, dims, deviation, reach, pieces=(), held_as=jnp.bfloat16):
    entries = jax.random.normal(stream_key, dims, jnp.float32) * deviation
    if len(pieces) > 0:
        entries = block_scale(stream_key, dims, pieces, -0.22, 0.18) * entries
    return jnp.clip(entries, min=-reach, max=reach).astype(held_as)


def noise_with(stream_key, shape, spread, reach, shards, heavy, kind=jnp.bfloat16):
    values = spread * jax.random.normal(stream_key, shape, jnp.float32)
    if shards:
        values = values * block_scale(stream_key, shape, shards, -0.22, 0.18)
    return jnp.clip(raised(values, jax.random.fold_in(stream_key, 3), *heavy), -reach, reach).astype(kind)


def setup_inputs(seed: int = 0) -> dict:
    key_of = jax.random.split(jax.random.key(seed), 5)
    gate_pre = normal_values(key_of[0], (TOKENS, FF), 1.5, 8.0, ((0, 4), (1, 8)))
    up_pre = normal_values(key_of[1], (TOKENS, FF), 1.0, 6.0, ((0, 4), (1, 8)))
    down_t = normal_values(key_of[2], (D, FF), D ** -0.5, 0.09375, ((0, 4), (1, 8)))
    grad_out = noise_with(key_of[3], (TOKENS, D), 1.0, 6.0, ((0, 4), (1, 8)), (0, 1, 8, 2.0))
    return dict(gate_pre=gate_pre, up_pre=up_pre, down_t=down_t, grad_out=grad_out)


def reference(gate_pre, up_pre, down_t, grad_out):
    gate_value = gate_pre.astype(jnp.float32)
    up_value = up_pre.astype(jnp.float32)
    gate_sigmoid = jax.nn.sigmoid(gate_value)
    activated = gate_value * gate_sigmoid
    hidden = (activated * up_value).astype(jnp.bfloat16)
    hidden_grad = jnp.dot(grad_out, down_t, preferred_element_type=jnp.float32)
    weight_sum = jnp.dot(grad_out.T, hidden, preferred_element_type=jnp.float32)
    weight_grad = (weight_sum * (TOKENS ** -0.5)).astype(jnp.bfloat16)
    up_grad = (hidden_grad * activated).astype(jnp.bfloat16)
    slope = gate_sigmoid * (1.0 + gate_value * (1.0 - gate_sigmoid))
    gate_grad = (hidden_grad * up_value * slope).astype(jnp.bfloat16)
    return gate_grad, up_grad, weight_grad
```

```python
import jax
import jax.numpy as jnp
from jax import lax
from jax.sharding import PartitionSpec as P

PARTS = 2


def spread_cotangent(grad_out):
    rows, cols = lax.axis_size("row"), lax.axis_size("col")
    per_row = cols // rows
    pairs = [
        (src * cols + per_row * dst + part, dst * cols + per_row * (src ^ dst) + part)
        for src in range(rows)
        for dst in range(rows)
        for part in range(per_row)
    ]
    moved = lax.ppermute(grad_out, ("row", "col"), pairs)
    blocks = lax.all_gather(moved, "col", axis=0)
    return blocks.reshape((rows, per_row) + grad_out.shape)


def per_device(gate_pre, up_pre, down_t, grad_out):
    rows = lax.axis_size("row")
    row = lax.axis_index("row")
    tok_rows, width = gate_pre.shape
    norm_scale = (tok_rows * rows) ** (-0.5)
    wire = jnp.bfloat16 if rows <= 4 else jnp.float32
    ahead = [(at, at + 1) for at in range(rows - 1)]
    behind = [(at + 1, at) for at in range(rows - 1)]

    blocks = spread_cotangent(grad_out)
    cot = blocks.transpose(0, 2, 1, 3).reshape(rows * tok_rows, -1)

    span = width // PARTS
    chains = []
    for part in range(PARTS):
        cut = slice(part * span, (part + 1) * span)
        gate_value = gate_pre[:, cut].astype(jnp.float32)
        up_value = up_pre[:, cut].astype(jnp.float32)
        hidden = (gate_value * jax.nn.sigmoid(gate_value) * up_value).astype(jnp.bfloat16)
        chains.append(
            dict(
                cut=cut,
                gate=gate_value,
                up=up_value,
                out=[hidden.astype(wire)] * 2,
                hidden=lax.dynamic_update_slice(
                    jnp.zeros((rows + 1, tok_rows, span), jnp.bfloat16), hidden[None], (0, 0, 0)
                ),
            )
        )
    for chain in chains:
        share = jnp.dot(cot, down_t[:, chain["cut"]], preferred_element_type=jnp.float32)
        chain["share"] = share.reshape(rows, tok_rows, span)

    for step in range(1, rows + 1):
        for chain in chains:
            fore = lax.ppermute(chain["out"][0], "row", ahead)
            back = lax.ppermute(chain["out"][1], "row", behind)
            chain["in"] = [fore, back]
            if step < rows:
                for got, owner, there in (
                    (fore, row - step, step <= row),
                    (back, row + step, step <= rows - 1 - row),
                ):
                    slot = jnp.where(there, owner ^ row, rows)
                    chain["hidden"] = lax.dynamic_update_slice(
                        chain["hidden"], got.astype(jnp.bfloat16)[None], (slot, 0, 0)
                    )
                nxt = step + 1
                for way, (target, mine) in enumerate(
                    (
                        (rows + 1 + row - nxt, nxt > row + 1),
                        (row + nxt - rows - 1, nxt > rows - row),
                    )
                ):
                    slot = jnp.where(mine, target, row) ^ row
                    share = lax.dynamic_index_in_dim(chain["share"], slot, 0, keepdims=False)
                    total = chain["in"][way].astype(jnp.float32) + jnp.where(mine, share, 0.0)
                    chain["out"][way] = total.astype(wire)

    gate_parts, up_parts, weight_parts = [], [], []
    for chain in chains:
        hidden_all = chain["hidden"][:rows].reshape(rows * tok_rows, span)
        weight_sum = lax.dot_general(
            cot, hidden_all, (((0,), (0,)), ((), ())), preferred_element_type=jnp.float32
        )
        weight_parts.append((weight_sum * norm_scale).astype(jnp.bfloat16))
        fore, back = (got.astype(jnp.float32) for got in chain["in"])
        hidden_grad = chain["share"][0] + fore + back
        gate_value, up_value = chain["gate"], chain["up"]
        gate_sigmoid = jax.nn.sigmoid(gate_value)
        up_parts.append((hidden_grad * (gate_value * gate_sigmoid)).astype(jnp.bfloat16))
        slope = gate_sigmoid * (1.0 + gate_value * (1.0 - gate_sigmoid))
        gate_parts.append((hidden_grad * up_value * slope).astype(jnp.bfloat16))
    return tuple(jnp.concatenate(parts, axis=1) for parts in (gate_parts, up_parts, weight_parts))


def solution(mesh):
    specs = (P("row", "col"),) * 4
    return jax.shard_map(
        per_device, mesh=mesh, in_specs=specs, out_specs=specs[:3], check_vma=False
    )
```

```python
import jax
import jax.numpy as jnp
from jax import lax
from jax.experimental import pallas as pl
from jax.experimental.pallas import tpu as pltpu
from jax.sharding import PartitionSpec as P

PARTS = 2


def after(value, first):
    return lax.optimization_barrier((value, first))[0]


def place_blocks(near_ref, far_ref, out_ref, sems):
    count, rows, strip, _ = near_ref.shape
    row, col = lax.axis_index("row"), lax.axis_index("col")
    copies = []
    for at in range(2 * count):
        ref, core = (near_ref, 0) if at < count else (far_ref, 1)
        owner = col ^ (2 * (at % count) + core)
        for group in range(rows):
            slot = lax.rem(group + rows - row, rows)
            start = (slot * 2 * count + owner) * strip
            dst = out_ref.at[pl.ds(pl.multiple_of(start, strip), strip)]
            copies.append(
                pltpu.make_async_copy(ref.at[at % count, group], dst, sems.at[at, group])
            )
    for copy in copies:
        copy.start()
    for copy in copies:
        copy.wait()


def spread_cotangent(grad_out, hidden):
    rows, cols = lax.axis_size("row"), lax.axis_size("col")
    tok_rows, width = grad_out.shape
    per_row = cols // rows
    if cols != 8:
        pairs = [
            (src * cols + per_row * dst + part, dst * cols + per_row * ((src - dst) % rows) + part)
            for src in range(rows)
            for dst in range(rows)
            for part in range(per_row)
        ]
        moved = lax.ppermute(grad_out, ("row", "col"), pairs)
        blocks = lax.all_gather(moved, "col", axis=0)
        blocks = blocks.reshape(rows, per_row, tok_rows, width)
        return blocks.transpose(0, 2, 1, 3).reshape(rows * tok_rows, per_row * width)
    strip = tok_rows // cols
    wide = lax.all_to_all(grad_out, "col", 0, 1, tiled=True)
    wide = after(wide, hidden)
    tall = lax.all_to_all(wide, "row", 1, 0, tiled=True)
    tall = tall.reshape(rows, strip, per_row * width)
    swap = lambda value, bits: lax.ppermute(value, "col", [(at, at ^ bits) for at in range(cols)])
    near = jnp.stack([tall, swap(tall, 2), swap(tall, 4), swap(tall, 6)])
    far = swap(near, 1)
    return pl.pallas_call(
        place_blocks,
        out_shape=jax.ShapeDtypeStruct((rows * tok_rows, per_row * width), grad_out.dtype),
        in_specs=[pl.BlockSpec(memory_space=pl.ANY)] * 2,
        out_specs=pl.BlockSpec(memory_space=pl.ANY),
        scratch_shapes=[pltpu.SemaphoreType.DMA((cols, rows))],
        name="place_blocks",
    )(near, far)


def per_device(gate_pre, up_pre, down_t, grad_out):
    rows = lax.axis_size("row")
    row = lax.axis_index("row")
    tok_rows, width = gate_pre.shape
    norm_scale = (tok_rows * rows) ** (-0.5)
    wire = jnp.bfloat16 if rows <= 4 else jnp.float32
    ahead = [(at, at + 1) for at in range(rows - 1)]
    behind = [(at + 1, at) for at in range(rows - 1)]

    gate_value = gate_pre.astype(jnp.float32)
    up_value = up_pre.astype(jnp.float32)
    hidden = (gate_value * jax.nn.sigmoid(gate_value) * up_value).astype(jnp.bfloat16)

    cot = spread_cotangent(grad_out, hidden)
    span = tok_rows // PARTS
    share = jnp.dot(cot, down_t, preferred_element_type=jnp.float32)
    share = share.reshape(rows, PARTS, span, width)

    out = [[hidden[at * span : (at + 1) * span].astype(wire)] * 2 for at in range(PARTS)]
    turn = hidden
    fore = [[None] for _ in range(PARTS)]
    back = [[None] for _ in range(PARTS)]
    for step in range(1, rows + 1):
        nxt = step + 1
        for at in range(PARTS):
            fore[at].append(lax.ppermute(out[at][0], "row", ahead))
            back[at].append(lax.ppermute(out[at][1], "row", behind))
            if step == rows:
                continue
            for way, (got, slot, mine) in enumerate(
                (
                    (fore[at][step], rows + 1 - nxt, nxt > row + 1),
                    (back[at][step], nxt - 1, nxt > rows - row),
                )
            ):
                got = after(got, turn)
                total = got.astype(jnp.float32) + jnp.where(mine, share[slot, at], 0.0)
                turn = out[at][way] = total.astype(wire)

    pieces = [hidden]
    for slot in range(1, rows):
        for at in range(PARTS):
            got = jnp.where(row + slot < rows, back[at][slot], fore[at][rows - slot])
            pieces.append(got.astype(jnp.bfloat16))
    weight_sum = lax.dot_general(
        cot,
        jnp.concatenate(pieces, axis=0),
        (((0,), (0,)), ((), ())),
        preferred_element_type=jnp.float32,
    )
    weight_grad = (weight_sum * norm_scale).astype(jnp.bfloat16)

    gate_parts, up_parts = [], []
    for at in range(PARTS):
        hidden_grad = (
            share[0, at]
            + fore[at][rows].astype(jnp.float32)
            + back[at][rows].astype(jnp.float32)
        )
        gate_cut = gate_value[at * span : (at + 1) * span]
        up_cut = up_value[at * span : (at + 1) * span]
        gate_sigmoid = jax.nn.sigmoid(gate_cut)
        up_parts.append((hidden_grad * (gate_cut * gate_sigmoid)).astype(jnp.bfloat16))
        slope = gate_sigmoid * (1.0 + gate_cut * (1.0 - gate_sigmoid))
        gate_parts.append((hidden_grad * up_cut * slope).astype(jnp.bfloat16))
    return jnp.concatenate(gate_parts), jnp.concatenate(up_parts), weight_grad


def solution(mesh):
    specs = (P("row", "col"),) * 4
    return jax.shard_map(
        per_device, mesh=mesh, in_specs=specs, out_specs=specs[:3], check_vma=False
    )
```

```python
import jax
import jax.numpy as jnp
from jax import lax
from jax.experimental import pallas as pl
from jax.experimental.pallas import tpu as pltpu
from jax.sharding import PartitionSpec as P

PARTS = 2


def after(value, first):
    return lax.optimization_barrier((value, first))[0]


def lay_strips(near, far, first=None):
    chips, groups, strip, width = near.shape
    tokens = 2 * chips * strip
    rows = groups if first is None else groups + 1

    def slot_of(group):
        row = lax.axis_index("row")
        return lax.rem((row ^ group) + rows - row, rows)

    def kernel(*refs):
        near_ref, far_ref, out_ref = refs[0], refs[1], refs[-1]
        col = lax.axis_index("col")
        for core, ref in enumerate((near_ref, far_ref)):
            for chip in range(chips):
                owner = col ^ (2 * chip + core)
                for group in range(groups):
                    slot = 0 if first is None else slot_of(group)
                    start = pl.multiple_of(slot * tokens + owner * strip, strip)
                    out_ref[pl.ds(start, strip), :] = ref[chip, group]
        if first is not None:
            start = pl.multiple_of(slot_of(rows - 1) * tokens, tokens)
            out_ref[pl.ds(start, tokens), :] = refs[2][...]

    operands = (near, far) if first is None else (near, far, first)
    return pl.pallas_call(
        kernel,
        out_shape=jax.ShapeDtypeStruct((rows * tokens, width), near.dtype),
        in_specs=[pl.BlockSpec(memory_space=pltpu.VMEM)] * len(operands),
        out_specs=pl.BlockSpec(memory_space=pltpu.VMEM),
        compiler_params=pltpu.CompilerParams(vmem_limit_bytes=32 * 2**20),
        name="lay_strips",
    )(*operands)


def swap(value, bits):
    return lax.ppermute(value, "col", [(at, at ^ bits) for at in range(lax.axis_size("col"))])


def over_chips(value):
    return [value, swap(value, 2), swap(value, 4), swap(value, 6)]


def with_core(values):
    near = jnp.stack(values)
    return near, swap(near, 1)


def spread_cotangent(grad_out, first):
    rows, cols = lax.axis_size("row"), lax.axis_size("col")
    row = lax.axis_index("row")
    tok_rows, width = grad_out.shape
    per_row = cols // rows
    if (rows, cols) != (4, 8):
        pairs = [
            (src * cols + per_row * dst + part, dst * cols + per_row * ((src - dst) % rows) + part)
            for src in range(rows)
            for dst in range(rows)
            for part in range(per_row)
        ]
        moved = lax.ppermute(grad_out, ("row", "col"), pairs)
        blocks = lax.all_gather(moved, "col", axis=0)
        blocks = blocks.reshape(rows, per_row, tok_rows, width)
        cot = blocks.transpose(0, 2, 1, 3).reshape(rows, tok_rows, per_row * width)
        return (cot[rows - 1], cot[1]), lambda first: cot.reshape(rows * tok_rows, -1)
    wide = lax.all_to_all(grad_out, "col", 0, 1, tiled=True)

    def across(bits):
        piece = lax.dynamic_slice_in_dim(wide, (row ^ bits) * per_row * width, per_row * width, 1)
        if bits == 0:
            return piece
        return lax.ppermute(piece, "row", [(at, at ^ bits) for at in range(rows)])

    others = jnp.stack([across(bits) for bits in range(rows - 1)])
    near_far = over_chips(across(rows - 1)[None])
    far_group = lay_strips(*with_core(after(near_far, (first, others))))
    near = over_chips(others)

    def rest(first):
        return lay_strips(*with_core(after(near, first)), far_group)

    return (far_group, far_group), rest


def per_device(gate_pre, up_pre, down_t, grad_out):
    rows = lax.axis_size("row")
    row = lax.axis_index("row")
    tok_rows, width = gate_pre.shape
    norm_scale = (tok_rows * rows) ** (-0.5)
    wire = jnp.bfloat16 if rows <= 4 else jnp.float32
    ahead = [(at, at + 1) for at in range(rows - 1)]
    behind = [(at + 1, at) for at in range(rows - 1)]
    span = tok_rows // PARTS

    def halves(value):
        return [value[at * span : (at + 1) * span] for at in range(PARTS)]

    gate_value = gate_pre.astype(jnp.float32)
    up_value = up_pre.astype(jnp.float32)
    hidden = (gate_value * jax.nn.sigmoid(gate_value) * up_value).astype(jnp.bfloat16)
    sent = hidden.astype(wire)
    fore = [None, [lax.ppermute(sent, "row", ahead)] * PARTS]
    back = [None, [lax.ppermute(sent, "row", behind)] * PARTS]

    firsts, rest = spread_cotangent(after(grad_out, hidden), (fore[1], back[1]))
    turn = hidden
    for step in range(2, rows + 1):
        fore.append([None] * PARTS)
        back.append([None] * PARTS)
        for at in range(PARTS):
            for way, (ends, slot, mine, pairs) in enumerate(
                ((fore, rows + 1 - step, step > row + 1, ahead), (back, step - 1, step > rows - row, behind))
            ):
                got = after(ends[step - 1][at], turn)
                if step == 2:
                    got = got[at * span : (at + 1) * span]
                    tokens = firsts[way][at * span : (at + 1) * span]
                else:
                    start = slot * tok_rows + at * span
                    tokens = cot[start : start + span]
                share = jnp.dot(tokens, down_t, preferred_element_type=jnp.float32)
                total = got.astype(jnp.float32) + jnp.where(mine, share, 0.0)
                turn = total.astype(wire)
                ends[step][at] = lax.ppermute(turn, "row", pairs)
            if step == 2 and at == 0:
                cot = rest(turn)
        late = turn

    pieces = [hidden]
    for slot in range(1, rows):
        for at in range(PARTS):
            ends = [back[slot][at], fore[rows - slot][at]]
            ends = [got[at * span : (at + 1) * span] if got.shape[0] == tok_rows else got for got in ends]
            pieces.append(jnp.where(row + slot < rows, *ends).astype(jnp.bfloat16))
    weight_sum = lax.dot_general(
        cot,
        jnp.concatenate(pieces, axis=0),
        (((0,), (0,)), ((), ())),
        preferred_element_type=jnp.float32,
    )
    weight_grad = (weight_sum * norm_scale).astype(jnp.bfloat16)

    own_share = jnp.dot(after(cot[:tok_rows], late), down_t, preferred_element_type=jnp.float32)
    own_share, gate_again, up_again = after((own_share, gate_pre, up_pre), turn)
    gate_parts, up_parts = [], []
    for share, gate_cut, up_cut, fore_sum, back_sum in zip(
        halves(own_share), halves(gate_again), halves(up_again), fore[rows], back[rows]
    ):
        hidden_grad = share + fore_sum.astype(jnp.float32) + back_sum.astype(jnp.float32)
        gate_cut = gate_cut.astype(jnp.float32)
        gate_sigmoid = jax.nn.sigmoid(gate_cut)
        up_parts.append((hidden_grad * (gate_cut * gate_sigmoid)).astype(jnp.bfloat16))
        slope = gate_sigmoid * (1.0 + gate_cut * (1.0 - gate_sigmoid))
        gate_parts.append((hidden_grad * up_cut.astype(jnp.float32) * slope).astype(jnp.bfloat16))
    return jnp.concatenate(gate_parts), jnp.concatenate(up_parts), weight_grad


def solution(mesh):
    specs = (P("row", "col"),) * 4
    return jax.shard_map(
        per_device, mesh=mesh, in_specs=specs, out_specs=specs[:3], check_vma=False
    )
```

```python
import jax
import jax.numpy as jnp
from jax import lax
from jax.experimental import pallas as pl
from jax.experimental.pallas import tpu as pltpu
from jax.sharding import PartitionSpec as P

PARTS = 2


def after(value, first):
    return lax.optimization_barrier((value, first))[0]


def lay_strips(near, far):
    chips, rows, strip, width = near.shape

    def kernel(near_ref, far_ref, out_ref):
        row, col = lax.axis_index("row"), lax.axis_index("col")
        for core, ref in enumerate((near_ref, far_ref)):
            for chip in range(chips):
                owner = col ^ (2 * chip + core)
                for group in range(rows):
                    slot = lax.rem((row ^ group) + rows - row, rows)
                    start = pl.multiple_of((slot * 2 * chips + owner) * strip, strip)
                    out_ref[pl.ds(start, strip), :] = ref[chip, group]

    return pl.pallas_call(
        kernel,
        out_shape=jax.ShapeDtypeStruct((rows * 2 * chips * strip, width), near.dtype),
        in_specs=[pl.BlockSpec(memory_space=pltpu.VMEM)] * 2,
        out_specs=pl.BlockSpec(memory_space=pltpu.VMEM),
        compiler_params=pltpu.CompilerParams(vmem_limit_bytes=32 * 2**20),
        name="lay_strips",
    )(near, far)


def swap(value, bits):
    return lax.ppermute(value, "col", [(at, at ^ bits) for at in range(lax.axis_size("col"))])


def spread_cotangent(grad_out, hidden, first):
    rows, cols = lax.axis_size("row"), lax.axis_size("col")
    row = lax.axis_index("row")
    tok_rows, width = grad_out.shape
    per_row = cols // rows
    if (rows, cols) != (4, 8):
        pairs = [
            (src * cols + per_row * dst + part, dst * cols + per_row * ((src - dst) % rows) + part)
            for src in range(rows)
            for dst in range(rows)
            for part in range(per_row)
        ]
        moved = lax.ppermute(grad_out, ("row", "col"), pairs)
        blocks = lax.all_gather(moved, "col", axis=0)
        blocks = blocks.reshape(rows, per_row, tok_rows, width)
        return blocks.transpose(0, 2, 1, 3).reshape(rows * tok_rows, per_row * width)
    wide = after(lax.all_to_all(grad_out, "col", 0, 1, tiled=True), hidden)

    def across(bits):
        piece = lax.dynamic_slice_in_dim(wide, (row ^ bits) * per_row * width, per_row * width, 1)
        if bits == 0:
            return piece
        return lax.ppermute(piece, "row", [(at, at ^ bits) for at in range(rows)])

    tall = [across(bits) for bits in range(rows - 1, -1, -1)]
    tall = jnp.stack(tall[::-1])
    near = jnp.stack([tall, swap(tall, 2), swap(tall, 4), swap(tall, 6)])
    return lay_strips(*after((near, swap(near, 1)), first))


def per_device(gate_pre, up_pre, down_t, grad_out):
    rows = lax.axis_size("row")
    row = lax.axis_index("row")
    tok_rows, width = gate_pre.shape
    norm_scale = (tok_rows * rows) ** (-0.5)
    wire = jnp.bfloat16 if rows <= 4 else jnp.float32
    ahead = [(at, at + 1) for at in range(rows - 1)]
    behind = [(at + 1, at) for at in range(rows - 1)]
    span = tok_rows // PARTS

    def halves(value):
        return [value[at * span : (at + 1) * span] for at in range(PARTS)]

    gate_value = gate_pre.astype(jnp.float32)
    activated = gate_value * jax.nn.sigmoid(gate_value)
    hidden = (activated * up_pre.astype(jnp.float32)).astype(jnp.bfloat16)
    fore = [None, [lax.ppermute(hidden.astype(wire), "row", ahead)] * PARTS]
    back = [None, [lax.ppermute(hidden.astype(wire), "row", behind)] * PARTS]

    cot = spread_cotangent(grad_out, hidden, (fore[1][0], back[1][0]))
    turn = hidden
    for step in range(2, rows + 1):
        fore.append([None] * PARTS)
        back.append([None] * PARTS)
        cot_now = after(cot, turn)
        for at in range(PARTS):
            for way, (ends, slot, mine, pairs) in enumerate(
                ((fore, rows + 1 - step, step > row + 1, ahead), (back, step - 1, step > rows - row, behind))
            ):
                got = after(ends[step - 1][at], turn)
                if step == 2:
                    got = halves(got)[at]
                start = slot * tok_rows + at * span
                share = jnp.dot(cot_now[start : start + span], down_t, preferred_element_type=jnp.float32)
                total = got.astype(jnp.float32) + jnp.where(mine, share, 0.0)
                turn = total.astype(wire)
                ends[step][at] = lax.ppermute(turn, "row", pairs)
        late = turn

    pieces = [after(hidden, turn)]
    for slot in range(1, rows):
        for at in range(PARTS):
            ends = [back[slot][at], fore[rows - slot][at]]
            ends = [got if got.shape[0] == span else halves(got)[at] for got in ends]
            pieces.append(jnp.where(row + slot < rows, *ends).astype(jnp.bfloat16))
    weight_sum = lax.dot_general(
        cot,
        jnp.concatenate(pieces, axis=0),
        (((0,), (0,)), ((), ())),
        preferred_element_type=jnp.float32,
    )
    weight_grad = (weight_sum * norm_scale).astype(jnp.bfloat16)

    own_share = jnp.dot(after(cot[:tok_rows], late), down_t, preferred_element_type=jnp.float32)
    own_share, gate_again, up_again = after((own_share, gate_pre, up_pre), turn)
    gate_grad = up_grad = jnp.zeros((tok_rows, width), jnp.bfloat16)
    for at in range(PARTS):
        share, gate_cut, up_cut = (halves(value)[at] for value in (own_share, gate_again, up_again))
        hidden_grad = share + fore[rows][at].astype(jnp.float32) + back[rows][at].astype(jnp.float32)
        gate_cut = gate_cut.astype(jnp.float32)
        gate_sigmoid = jax.nn.sigmoid(gate_cut)
        up_part = (hidden_grad * (gate_cut * gate_sigmoid)).astype(jnp.bfloat16)
        slope = gate_sigmoid * (1.0 + gate_cut * (1.0 - gate_sigmoid))
        gate_part = (hidden_grad * up_cut.astype(jnp.float32) * slope).astype(jnp.bfloat16)
        gate_grad = lax.dynamic_update_slice(gate_grad, gate_part, (at * span, 0))
        up_grad = lax.dynamic_update_slice(up_grad, up_part, (at * span, 0))
        if at < PARTS - 1:
            gate_grad, up_grad = lax.optimization_barrier((gate_grad, up_grad))
    return gate_grad, up_grad, weight_grad


def solution(mesh):
    specs = (P("row", "col"),) * 4
    return jax.shard_map(
        per_device, mesh=mesh, in_specs=specs, out_specs=specs[:3], check_vma=False
    )
```

```python
import jax
import jax.numpy as jnp
from jax import lax
from jax.experimental import pallas as pl
from jax.experimental.pallas import tpu as pltpu
from jax.sharding import PartitionSpec as P

PARTS = 2


def after(value, first):
    return lax.optimization_barrier((value, first))[0]


def lay_strips(near, far):
    chips, rows, strip, width = near.shape

    def kernel(near_ref, far_ref, out_ref):
        row, col = lax.axis_index("row"), lax.axis_index("col")
        for at, ref in enumerate((near_ref, far_ref)):
            lane = pl.multiple_of(((col & 1) ^ at) * width, width)
            for chip in range(chips):
                for group in range(rows):
                    slot = lax.rem((row ^ group) + rows - row, rows)
                    start = (slot * chips + (col // 2 ^ chip)) * strip
                    out_ref[pl.ds(pl.multiple_of(start, strip), strip), pl.ds(lane, width)] = ref[chip, group]

    return pl.pallas_call(
        kernel,
        out_shape=jax.ShapeDtypeStruct((rows * chips * strip, 2 * width), near.dtype),
        in_specs=[pl.BlockSpec(memory_space=pltpu.VMEM)] * 2,
        out_specs=pl.BlockSpec(memory_space=pltpu.VMEM),
        compiler_params=pltpu.CompilerParams(vmem_limit_bytes=32 * 2**20),
        name="lay_strips",
    )(near, far)


def add_share(got, cot, down_t, start, mine):
    span, width = got.shape
    tile = 512 if width % 512 == 0 else width

    def kernel(got_ref, cot_ref, down_ref, out_ref):
        is_sum = mine(lax.axis_index("row"))

        @pl.when(is_sum)
        def _():
            tokens = cot_ref[start : start + span, :]
            for at in range(0, width, tile):
                share = jnp.dot(tokens, down_ref[:, at : at + tile], preferred_element_type=jnp.float32)
                total = got_ref[:, at : at + tile].astype(jnp.float32) + share
                out_ref[:, at : at + tile] = total.astype(out_ref.dtype)

        @pl.when(jnp.logical_not(is_sum))
        def _():
            out_ref[...] = got_ref[...]

    whole = pl.BlockSpec(memory_space=pltpu.VMEM)
    return pl.pallas_call(
        kernel,
        out_shape=jax.ShapeDtypeStruct(got.shape, got.dtype),
        in_specs=[whole] * 3,
        out_specs=whole,
        compiler_params=pltpu.CompilerParams(vmem_limit_bytes=32 * 2**20),
        cost_estimate=pl.CostEstimate(
            flops=2 * span * down_t.size, bytes_accessed=2 * got.nbytes, transcendentals=0
        ),
        name="add_share",
    )(got, cot, down_t)


def weight_product(cot, own, fore, back, scale):
    rows, parts = len(fore) + 1, len(fore[0])
    tok_rows, width = own.shape
    span = tok_rows // parts
    tile = 512 if width % 512 == 0 else width
    flat = [piece for pieces in fore + back for piece in pieces]

    def kernel(cot_ref, own_ref, *refs):
        ends, out_ref, hidden_ref = refs[: len(flat)], refs[len(flat)], refs[len(flat) + 1]
        row = lax.axis_index("row")

        def place(end, start, cut):
            rows_here = pl.ds(start, end.shape[0])
            hidden_ref[rows_here, :] = end[:, cut].astype(hidden_ref.dtype)

        @pl.loop(0, width // tile)
        def _(at):
            cut = pl.ds(pl.multiple_of(at * tile, tile), tile)
            hidden_ref[:tok_rows, :] = own_ref[:, cut]
            for slot in range(1, rows):
                for part in range(parts):
                    ahead = ends[(rows - slot - 1) * parts + part]
                    behind = ends[(rows - 1 + slot - 1) * parts + part]
                    start = slot * tok_rows + part * span
                    pl.when(row + slot < rows)(lambda end=behind, start=start: place(end, start, cut))
                    pl.when(row + slot >= rows)(lambda end=ahead, start=start: place(end, start, cut))
            total = lax.dot_general(
                cot_ref[...],
                hidden_ref[...],
                (((0,), (0,)), ((), ())),
                preferred_element_type=jnp.float32,
            )
            out_ref[:, cut] = (total * scale).astype(out_ref.dtype)

    whole = pl.BlockSpec(memory_space=pltpu.VMEM)
    return pl.pallas_call(
        kernel,
        out_shape=jax.ShapeDtypeStruct((cot.shape[1], width), jnp.bfloat16),
        in_specs=[whole] * (2 + len(flat)),
        out_specs=whole,
        scratch_shapes=[pltpu.VMEM((cot.shape[0], tile), jnp.bfloat16)],
        compiler_params=pltpu.CompilerParams(vmem_limit_bytes=32 * 2**20),
        cost_estimate=pl.CostEstimate(
            flops=2 * cot.size * width, bytes_accessed=4 * cot.shape[0] * width, transcendentals=0
        ),
        name="weight_product",
    )(cot, own, *flat)


def swap(value, bits):
    return lax.ppermute(value, "col", [(at, at ^ bits) for at in range(lax.axis_size("col"))])


def spread_cotangent(grad_out, hidden, first):
    rows, cols = lax.axis_size("row"), lax.axis_size("col")
    row = lax.axis_index("row")
    tok_rows, width = grad_out.shape
    per_row = cols // rows
    if (rows, cols) != (4, 8):
        pairs = [
            (src * cols + per_row * dst + part, dst * cols + per_row * ((src - dst) % rows) + part)
            for src in range(rows)
            for dst in range(rows)
            for part in range(per_row)
        ]
        moved = lax.ppermute(grad_out, ("row", "col"), pairs)
        blocks = lax.all_gather(moved, "col", axis=0)
        blocks = blocks.reshape(rows, per_row, tok_rows, width)
        return blocks.transpose(0, 2, 1, 3).reshape(rows * tok_rows, per_row * width)
    strip = tok_rows * 2 // cols
    chip = lax.axis_index("col") // 2

    def quarter(bits):
        piece = lax.dynamic_slice_in_dim(grad_out, (chip ^ bits) * strip, strip, 0)
        return swap(piece, 2 * bits) if bits else piece

    wide = after([quarter(bits) for bits in range(cols // 2)], hidden[0])

    def across(bits):
        piece = lax.dynamic_index_in_dim(jnp.stack(wide), chip ^ row ^ bits, 0, keepdims=False)
        return lax.ppermute(piece, "row", [(at, at ^ bits) for at in range(rows)]) if bits else piece

    tall = [across(bits) for bits in range(rows - 1, -1, -1)]
    tall = jnp.stack(tall[::-1])
    near = jnp.stack([tall, swap(tall, 2), swap(tall, 4), swap(tall, 6)])
    near = after(near, first)
    return lay_strips(near, swap(near, 1))


def per_device(gate_pre, up_pre, down_t, grad_out):
    rows = lax.axis_size("row")
    row = lax.axis_index("row")
    tok_rows, width = gate_pre.shape
    norm_scale = (tok_rows * rows) ** (-0.5)
    wire = jnp.bfloat16 if rows <= 4 else jnp.float32
    ahead = [(at, at + 1) for at in range(rows - 1)]
    behind = [(at + 1, at) for at in range(rows - 1)]
    span = tok_rows // PARTS

    def halves(value):
        return [value[at * span : (at + 1) * span] for at in range(PARTS)]

    hidden, fore, back = [], [None, []], [None, []]
    for gate_cut, up_cut in zip(halves(gate_pre), halves(up_pre)):
        gate_cut = gate_cut.astype(jnp.float32)
        activated = gate_cut * jax.nn.sigmoid(gate_cut)
        hidden.append((activated * up_cut.astype(jnp.float32)).astype(jnp.bfloat16))
        fore[1].append(lax.ppermute(hidden[-1].astype(wire), "row", ahead))
        back[1].append(lax.ppermute(hidden[-1].astype(wire), "row", behind))

    cot = spread_cotangent(grad_out, hidden, (fore[1][0], back[1][0]))
    turn = hidden[0]
    for step in range(2, rows + 1):
        fore.append([None] * PARTS)
        back.append([None] * PARTS)
        for at in range(PARTS):
            for ends, slot, mine, pairs in (
                (fore, rows + 1 - step, lambda row, step=step: step > row + 1, ahead),
                (back, step - 1, lambda row, step=step: step > rows - row, behind),
            ):
                got = after(ends[step - 1][at], turn)
                turn = add_share(got, cot, down_t, slot * tok_rows + at * span, mine)
                ends[step][at] = lax.ppermute(turn, "row", pairs)
        late = turn

    weight_grad = weight_product(cot, jnp.concatenate(hidden), fore[1:rows], back[1:rows], norm_scale)

    own_share = jnp.dot(after(cot[:tok_rows], late), down_t, preferred_element_type=jnp.float32)
    own_share, gate_again, up_again = after((own_share, gate_pre, up_pre), turn)
    gate_grad = up_grad = jnp.zeros((tok_rows, width), jnp.bfloat16)
    for at in range(PARTS):
        share, gate_cut, up_cut = (halves(value)[at] for value in (own_share, gate_again, up_again))
        hidden_grad = share + fore[rows][at].astype(jnp.float32) + back[rows][at].astype(jnp.float32)
        gate_cut = gate_cut.astype(jnp.float32)
        gate_sigmoid = jax.nn.sigmoid(gate_cut)
        up_part = (hidden_grad * (gate_cut * gate_sigmoid)).astype(jnp.bfloat16)
        slope = gate_sigmoid * (1.0 + gate_cut * (1.0 - gate_sigmoid))
        gate_part = (hidden_grad * up_cut.astype(jnp.float32) * slope).astype(jnp.bfloat16)
        gate_grad = lax.dynamic_update_slice(gate_grad, gate_part, (at * span, 0))
        up_grad = lax.dynamic_update_slice(up_grad, up_part, (at * span, 0))
        if at < PARTS - 1:
            gate_grad, up_grad = lax.optimization_barrier((gate_grad, up_grad))
    return gate_grad, up_grad, weight_grad


def solution(mesh):
    specs = (P("row", "col"),) * 4
    return jax.shard_map(
        per_device, mesh=mesh, in_specs=specs, out_specs=specs[:3], check_vma=False
    )
```

```python
import jax
import jax.numpy as jnp
from jax import lax
from jax.experimental import pallas as pl
from jax.experimental.pallas import tpu as pltpu
from jax.sharding import PartitionSpec as P

PARTS = 2


def after(value, first):
    return lax.optimization_barrier((value, first))[0]


def lay_strips(near, far):
    chips, rows, strip, width = near.shape

    def kernel(near_ref, far_ref, out_ref):
        row, col = lax.axis_index("row"), lax.axis_index("col")
        for at, ref in enumerate((near_ref, far_ref)):
            lane = pl.multiple_of(((col & 1) ^ at) * width, width)
            for chip in range(chips):
                for group in range(rows):
                    slot = lax.rem((row ^ group) + rows - row, rows)
                    start = (slot * chips + (col // 2 ^ chip)) * strip
                    out_ref[pl.ds(pl.multiple_of(start, strip), strip), pl.ds(lane, width)] = ref[chip, group]

    return pl.pallas_call(
        kernel,
        out_shape=jax.ShapeDtypeStruct((rows * chips * strip, 2 * width), near.dtype),
        in_specs=[pl.BlockSpec(memory_space=pltpu.VMEM)] * 2,
        out_specs=pl.BlockSpec(memory_space=pltpu.VMEM),
        compiler_params=pltpu.CompilerParams(vmem_limit_bytes=32 * 2**20),
        name="lay_strips",
    )(near, far)


def add_share(sources, cot, down_t, start, mine):
    span = sum(count for _, _, count in sources)
    like = sources[0][0]
    width = like.shape[1]
    tile = 512 if width % 512 == 0 else width

    def kernel(*refs):
        got_refs, (cot_ref, down_ref, out_ref) = refs[: len(sources)], refs[len(sources) :]
        is_sum = mine(lax.axis_index("row"))
        places, at = [], 0
        for ref, (_, first, count) in zip(got_refs, sources):
            places.append((ref, slice(first, first + count), slice(at, at + count)))
            at += count

        @pl.when(is_sum)
        def _():
            tokens = cot_ref[start : start + span, :]
            for at in range(0, width, tile):
                cut = slice(at, at + tile)
                share = jnp.dot(tokens, down_ref[:, cut], preferred_element_type=jnp.float32)
                for ref, source, here in places:
                    total = ref[source, cut].astype(jnp.float32) + share[here]
                    out_ref[here, cut] = total.astype(out_ref.dtype)

        @pl.when(jnp.logical_not(is_sum))
        def _():
            for ref, source, here in places:
                out_ref[here, :] = ref[source, :]

    whole = pl.BlockSpec(memory_space=pltpu.VMEM)
    return pl.pallas_call(
        kernel,
        out_shape=jax.ShapeDtypeStruct((span, width), like.dtype),
        in_specs=[whole] * (2 + len(sources)),
        out_specs=whole,
        compiler_params=pltpu.CompilerParams(vmem_limit_bytes=32 * 2**20),
        cost_estimate=pl.CostEstimate(
            flops=2 * span * down_t.size, bytes_accessed=4 * span * width, transcendentals=0
        ),
        name="add_share",
    )(*(array for array, _, _ in sources), cot, down_t)


def rows_of(pieces, start, count):
    found, at = [], 0
    for piece in pieces:
        low, high = max(start, at), min(start + count, at + piece.shape[0])
        if low < high:
            found.append((piece, low - at, high - low))
        at += piece.shape[0]
    return found


def weight_product(cot, own, fore, back, scale):
    rows = len(fore) + 1
    tok_rows, width = own.shape
    tile = 512 if width % 512 == 0 else width
    flat = [piece for pieces in fore + back for piece in pieces]

    def kernel(cot_ref, own_ref, *refs):
        ends, (out_ref, hidden_ref) = iter(refs[: len(flat)]), refs[len(flat) :]
        fore_refs, back_refs = ([[next(ends) for _ in pieces] for pieces in way] for way in (fore, back))
        row = lax.axis_index("row")

        def place(pieces, start, cut):
            for piece in pieces:
                hidden_ref[start : start + piece.shape[0], :] = piece[:, cut].astype(hidden_ref.dtype)
                start += piece.shape[0]

        @pl.loop(0, width // tile)
        def _(at):
            cut = pl.ds(pl.multiple_of(at * tile, tile), tile)
            place([own_ref], 0, cut)
            for slot in range(1, rows):
                for here, pieces in (
                    (row + slot < rows, back_refs[slot - 1]),
                    (row + slot >= rows, fore_refs[rows - slot - 1]),
                ):
                    pl.when(here)(lambda pieces=pieces, slot=slot: place(pieces, slot * tok_rows, cut))
            total = lax.dot_general(
                cot_ref[...],
                hidden_ref[...],
                (((0,), (0,)), ((), ())),
                preferred_element_type=jnp.float32,
            )
            out_ref[:, cut] = (total * scale).astype(out_ref.dtype)

    whole = pl.BlockSpec(memory_space=pltpu.VMEM)
    return pl.pallas_call(
        kernel,
        out_shape=jax.ShapeDtypeStruct((cot.shape[1], width), jnp.bfloat16),
        in_specs=[whole] * (2 + len(flat)),
        out_specs=whole,
        scratch_shapes=[pltpu.VMEM((cot.shape[0], tile), jnp.bfloat16)],
        compiler_params=pltpu.CompilerParams(vmem_limit_bytes=32 * 2**20),
        cost_estimate=pl.CostEstimate(
            flops=2 * cot.size * width, bytes_accessed=4 * cot.shape[0] * width, transcendentals=0
        ),
        name="weight_product",
    )(cot, own, *flat)


def finish(gate_pre, up_pre, share, fore, back, start, grads):
    span, width = fore.shape
    tile = 512 if width % 512 == 0 else width
    old = () if grads is None else tuple(grads)

    def kernel(*refs):
        gate_ref, up_ref, share_ref, fore_ref, back_ref = refs[:5]
        outs, parts, sems = refs[5 + len(old) : 7 + len(old)], refs[-3:-1], refs[-1]
        here = slice(start, start + span)
        copies = []
        for at in range(0, width, tile):
            cut = slice(at, at + tile)
            grad = share_ref[here, cut] + fore_ref[:, cut].astype(jnp.float32) + back_ref[:, cut].astype(jnp.float32)
            gate = gate_ref[here, cut].astype(jnp.float32)
            sigmoid = jax.nn.sigmoid(gate)
            slope = sigmoid * (1.0 + gate * (1.0 - sigmoid))
            parts[0][:, cut] = (grad * up_ref[here, cut].astype(jnp.float32) * slope).astype(jnp.bfloat16)
            parts[1][:, cut] = (grad * (gate * sigmoid)).astype(jnp.bfloat16)
            for which, (part, out) in enumerate(zip(parts, outs)):
                copy = pltpu.make_async_copy(part.at[:, cut], out.at[here, cut], sems.at[which, at // tile])
                copy.start()
                copies.append(copy)
        for copy in copies:
            copy.wait()

    whole, anywhere = pl.BlockSpec(memory_space=pltpu.VMEM), pl.BlockSpec(memory_space=pl.ANY)
    return pl.pallas_call(
        kernel,
        out_shape=[jax.ShapeDtypeStruct(gate_pre.shape, jnp.bfloat16)] * 2,
        in_specs=[whole] * 5 + [anywhere] * len(old),
        out_specs=[anywhere] * 2,
        scratch_shapes=[pltpu.VMEM((span, width), jnp.bfloat16)] * 2
        + [pltpu.SemaphoreType.DMA((2, width // tile))],
        input_output_aliases={5 + at: at for at in range(len(old))},
        compiler_params=pltpu.CompilerParams(vmem_limit_bytes=32 * 2**20),
        cost_estimate=pl.CostEstimate(flops=20 * span * width, bytes_accessed=8 * span * width, transcendentals=span * width),
        name="finish",
    )(gate_pre, up_pre, share, fore, back, *old)


def swap(value, bits):
    return lax.ppermute(value, "col", [(at, at ^ bits) for at in range(lax.axis_size("col"))])


def spread_cotangent(grad_out, hidden, first):
    rows, cols = lax.axis_size("row"), lax.axis_size("col")
    row = lax.axis_index("row")
    tok_rows, width = grad_out.shape
    per_row = cols // rows
    if (rows, cols) != (4, 8):
        pairs = [
            (src * cols + per_row * dst + part, dst * cols + per_row * ((src - dst) % rows) + part)
            for src in range(rows)
            for dst in range(rows)
            for part in range(per_row)
        ]
        moved = lax.ppermute(grad_out, ("row", "col"), pairs)
        blocks = lax.all_gather(moved, "col", axis=0)
        blocks = blocks.reshape(rows, per_row, tok_rows, width)
        return blocks.transpose(0, 2, 1, 3).reshape(rows * tok_rows, per_row * width)
    strip = tok_rows * 2 // cols
    chip = lax.axis_index("col") // 2

    def quarter(bits):
        piece = lax.dynamic_slice_in_dim(grad_out, (chip ^ bits) * strip, strip, 0)
        return swap(piece, 2 * bits) if bits else piece

    wide = after([quarter(bits) for bits in range(cols // 2)], hidden[0])

    def across(bits):
        piece = lax.dynamic_index_in_dim(jnp.stack(wide), chip ^ row ^ bits, 0, keepdims=False)
        return lax.ppermute(piece, "row", [(at, at ^ bits) for at in range(rows)]) if bits else piece

    tall = [across(bits) for bits in range(rows - 1, -1, -1)]
    tall = jnp.stack(tall[::-1])
    near = jnp.stack([tall, swap(tall, 2), swap(tall, 4), swap(tall, 6)])
    near = after(near, first)
    return lay_strips(near, swap(near, 1))


def per_device(gate_pre, up_pre, down_t, grad_out):
    rows = lax.axis_size("row")
    row = lax.axis_index("row")
    tok_rows, width = gate_pre.shape
    norm_scale = (tok_rows * rows) ** (-0.5)
    wire = jnp.bfloat16 if rows <= 4 else jnp.float32
    ahead = [(at, at + 1) for at in range(rows - 1)]
    behind = [(at + 1, at) for at in range(rows - 1)]
    span = tok_rows // PARTS

    hidden, fore, back = [], [None, []], [None, []]
    for start, count in ((0, span), (span, span // 2), (span + span // 2, span // 2)):
        gate_cut = gate_pre[start : start + count].astype(jnp.float32)
        up_cut = up_pre[start : start + count].astype(jnp.float32)
        hidden.append((gate_cut * jax.nn.sigmoid(gate_cut) * up_cut).astype(jnp.bfloat16))
        fore[1].append(lax.ppermute(hidden[-1].astype(wire), "row", ahead))
        back[1].append(lax.ppermute(hidden[-1].astype(wire), "row", behind))

    cot = spread_cotangent(grad_out, hidden, (fore[1][:2], back[1][:2]))
    turn = hidden[0]
    for step in range(2, rows + 1):
        fore.append([None] * PARTS)
        back.append([None] * PARTS)
        for at in range(PARTS):
            for ends, slot, mine, pairs in (
                (fore, rows + 1 - step, lambda row, step=step: step > row + 1, ahead),
                (back, step - 1, lambda row, step=step: step > rows - row, behind),
            ):
                sources = [
                    (after(piece, turn), first, count)
                    for piece, first, count in rows_of(ends[step - 1], at * span, span)
                ]
                turn = add_share(sources, cot, down_t, slot * tok_rows + at * span, mine)
                ends[step][at] = lax.ppermute(turn, "row", pairs)
        late = turn

    weight_grad = weight_product(cot, jnp.concatenate(hidden), fore[1:rows], back[1:rows], norm_scale)

    own_share = jnp.dot(after(cot[:tok_rows], late), down_t, preferred_element_type=jnp.float32)
    own_share, gate_again, up_again = after((own_share, gate_pre, up_pre), turn)
    grads = None
    for at in range(PARTS):
        grads = finish(gate_again, up_again, own_share, fore[rows][at], back[rows][at], at * span, grads)
    return *grads, weight_grad


def solution(mesh):
    specs = (P("row", "col"),) * 4
    return jax.shard_map(
        per_device, mesh=mesh, in_specs=specs, out_specs=specs[:3], check_vma=False
    )
```

```python
import jax
import jax.numpy as jnp
from jax import lax
from jax.experimental import pallas as pl
from jax.experimental.pallas import tpu as pltpu
from jax.sharding import PartitionSpec as P

PARTS = 2


def after(value, first):
    return lax.optimization_barrier((value, first))[0]


def lay_strips(near, far):
    chips = len(near)
    rows, strip, width = near[0].shape

    def kernel(*refs):
        row, col = lax.axis_index("row"), lax.axis_index("col")
        out_ref = refs[-1]
        for at, ref in enumerate(refs[:-1]):
            core, chip = at // chips, at % chips
            lane = pl.multiple_of(((col & 1) ^ core) * width, width)
            for group in range(rows):
                slot = lax.rem((row ^ group) + rows - row, rows)
                start = (slot * chips + (col // 2 ^ chip)) * strip
                out_ref[pl.ds(pl.multiple_of(start, strip), strip), pl.ds(lane, width)] = ref[group]

    return pl.pallas_call(
        kernel,
        out_shape=jax.ShapeDtypeStruct((rows * chips * strip, 2 * width), near[0].dtype),
        in_specs=[pl.BlockSpec(memory_space=pltpu.VMEM)] * 2 * chips,
        out_specs=pl.BlockSpec(memory_space=pltpu.VMEM),
        compiler_params=pltpu.CompilerParams(vmem_limit_bytes=32 * 2**20),
        name="lay_strips",
    )(*near, *far)


def add_share(sources, cot, down_t, start, mine):
    span = sum(count for _, _, count in sources)
    like = sources[0][0]
    width = like.shape[1]
    tile = 512 if width % 512 == 0 else width

    def kernel(*refs):
        got_refs, (cot_ref, down_ref, out_ref) = refs[: len(sources)], refs[len(sources) :]
        is_sum = mine(lax.axis_index("row"))
        places, at = [], 0
        for ref, (_, first, count) in zip(got_refs, sources):
            places.append((ref, slice(first, first + count), slice(at, at + count)))
            at += count

        @pl.when(is_sum)
        def _():
            tokens = cot_ref[start : start + span, :]
            for at in range(0, width, tile):
                cut = slice(at, at + tile)
                share = jnp.dot(tokens, down_ref[:, cut], preferred_element_type=jnp.float32)
                for ref, source, here in places:
                    total = ref[source, cut].astype(jnp.float32) + share[here]
                    out_ref[here, cut] = total.astype(out_ref.dtype)

        @pl.when(jnp.logical_not(is_sum))
        def _():
            for ref, source, here in places:
                out_ref[here, :] = ref[source, :]

    whole = pl.BlockSpec(memory_space=pltpu.VMEM)
    return pl.pallas_call(
        kernel,
        out_shape=jax.ShapeDtypeStruct((span, width), like.dtype),
        in_specs=[whole] * (2 + len(sources)),
        out_specs=whole,
        compiler_params=pltpu.CompilerParams(vmem_limit_bytes=32 * 2**20),
        cost_estimate=pl.CostEstimate(
            flops=2 * span * down_t.size, bytes_accessed=4 * span * width, transcendentals=0
        ),
        name="add_share",
    )(*(array for array, _, _ in sources), cot, down_t)


def rows_of(pieces, start, count):
    found, at = [], 0
    for piece in pieces:
        low, high = max(start, at), min(start + count, at + piece.shape[0])
        if low < high:
            found.append((piece, low - at, high - low))
        at += piece.shape[0]
    return found


def weight_product(cot, own, fore, back, scale):
    rows = len(fore) + 1
    tok_rows, width = own.shape
    tile = 512 if width % 512 == 0 else width
    flat = [piece for pieces in fore + back for piece in pieces]

    def kernel(cot_ref, own_ref, *refs):
        ends, (out_ref, hidden_ref) = iter(refs[: len(flat)]), refs[len(flat) :]
        fore_refs, back_refs = ([[next(ends) for _ in pieces] for pieces in way] for way in (fore, back))
        row = lax.axis_index("row")

        def place(pieces, start, cut):
            for piece in pieces:
                hidden_ref[start : start + piece.shape[0], :] = piece[:, cut].astype(hidden_ref.dtype)
                start += piece.shape[0]

        @pl.loop(0, width // tile)
        def _(at):
            cut = pl.ds(pl.multiple_of(at * tile, tile), tile)
            place([own_ref], 0, cut)
            for slot in range(1, rows):
                for here, pieces in (
                    (row + slot < rows, back_refs[slot - 1]),
                    (row + slot >= rows, fore_refs[rows - slot - 1]),
                ):
                    pl.when(here)(lambda pieces=pieces, slot=slot: place(pieces, slot * tok_rows, cut))
            total = lax.dot_general(
                cot_ref[...],
                hidden_ref[...],
                (((0,), (0,)), ((), ())),
                preferred_element_type=jnp.float32,
            )
            out_ref[:, cut] = (total * scale).astype(out_ref.dtype)

    whole = pl.BlockSpec(memory_space=pltpu.VMEM)
    return pl.pallas_call(
        kernel,
        out_shape=jax.ShapeDtypeStruct((cot.shape[1], width), jnp.bfloat16),
        in_specs=[whole] * (2 + len(flat)),
        out_specs=whole,
        scratch_shapes=[pltpu.VMEM((cot.shape[0], tile), jnp.bfloat16)],
        compiler_params=pltpu.CompilerParams(vmem_limit_bytes=32 * 2**20),
        cost_estimate=pl.CostEstimate(
            flops=2 * cot.size * width, bytes_accessed=4 * cot.shape[0] * width, transcendentals=0
        ),
        name="weight_product",
    )(cot, own, *flat)


def finish(gate_pre, up_pre, share, fore, back, start, grads):
    span, width = fore.shape
    tile = 512 if width % 512 == 0 else width
    old = () if grads is None else tuple(grads)

    def kernel(*refs):
        gate_ref, up_ref, share_ref, fore_ref, back_ref = refs[:5]
        outs, parts, sems = refs[5 + len(old) : 7 + len(old)], refs[-3:-1], refs[-1]
        here = slice(start, start + span)
        copies = []
        for at in range(0, width, tile):
            cut = slice(at, at + tile)
            grad = share_ref[here, cut] + fore_ref[:, cut].astype(jnp.float32) + back_ref[:, cut].astype(jnp.float32)
            gate = gate_ref[here, cut].astype(jnp.float32)
            sigmoid = jax.nn.sigmoid(gate)
            slope = sigmoid * (1.0 + gate * (1.0 - sigmoid))
            parts[0][:, cut] = (grad * up_ref[here, cut].astype(jnp.float32) * slope).astype(jnp.bfloat16)
            parts[1][:, cut] = (grad * (gate * sigmoid)).astype(jnp.bfloat16)
            for which, (part, out) in enumerate(zip(parts, outs)):
                copy = pltpu.make_async_copy(part.at[:, cut], out.at[here, cut], sems.at[which, at // tile])
                copy.start()
                copies.append(copy)
        for copy in copies:
            copy.wait()

    whole, anywhere = pl.BlockSpec(memory_space=pltpu.VMEM), pl.BlockSpec(memory_space=pl.ANY)
    return pl.pallas_call(
        kernel,
        out_shape=[jax.ShapeDtypeStruct(gate_pre.shape, jnp.bfloat16)] * 2,
        in_specs=[whole] * 5 + [anywhere] * len(old),
        out_specs=[anywhere] * 2,
        scratch_shapes=[pltpu.VMEM((span, width), jnp.bfloat16)] * 2
        + [pltpu.SemaphoreType.DMA((2, width // tile))],
        input_output_aliases={5 + at: at for at in range(len(old))},
        compiler_params=pltpu.CompilerParams(vmem_limit_bytes=32 * 2**20),
        cost_estimate=pl.CostEstimate(flops=20 * span * width, bytes_accessed=8 * span * width, transcendentals=span * width),
        name="finish",
    )(gate_pre, up_pre, share, fore, back, *old)


def swap(value, bits):
    return lax.ppermute(value, "col", [(at, at ^ bits) for at in range(lax.axis_size("col"))])


def spread_cotangent(grad_out, hidden, first):
    rows, cols = lax.axis_size("row"), lax.axis_size("col")
    row = lax.axis_index("row")
    tok_rows, width = grad_out.shape
    per_row = cols // rows
    if (rows, cols) != (4, 8):
        pairs = [
            (src * cols + per_row * dst + part, dst * cols + per_row * ((src - dst) % rows) + part)
            for src in range(rows)
            for dst in range(rows)
            for part in range(per_row)
        ]
        moved = lax.ppermute(grad_out, ("row", "col"), pairs)
        blocks = lax.all_gather(moved, "col", axis=0)
        blocks = blocks.reshape(rows, per_row, tok_rows, width)
        return blocks.transpose(0, 2, 1, 3).reshape(rows * tok_rows, per_row * width)
    strip = tok_rows * 2 // cols
    chip = lax.axis_index("col") // 2

    def quarter(bits):
        piece = lax.dynamic_slice_in_dim(grad_out, (chip ^ bits) * strip, strip, 0)
        return swap(piece, 2 * bits) if bits else piece

    wide = after([quarter(bits) for bits in range(cols // 2)], hidden[0])

    def across(bits):
        piece = lax.dynamic_index_in_dim(jnp.stack(wide), chip ^ row ^ bits, 0, keepdims=False)
        return lax.ppermute(piece, "row", [(at, at ^ bits) for at in range(rows)]) if bits else piece

    tall = [across(bits) for bits in range(rows - 1, -1, -1)]
    tall = jnp.stack(tall[::-1])
    near = [tall, swap(tall, 2), swap(tall, 4), swap(tall, 6)]
    near[-1] = after(near[-1], first)
    return lay_strips(near, [swap(block, 1) for block in near])


def per_device(gate_pre, up_pre, down_t, grad_out):
    rows = lax.axis_size("row")
    row = lax.axis_index("row")
    tok_rows, width = gate_pre.shape
    norm_scale = (tok_rows * rows) ** (-0.5)
    wire = jnp.bfloat16 if rows <= 4 else jnp.float32
    ahead = [(at, at + 1) for at in range(rows - 1)]
    behind = [(at + 1, at) for at in range(rows - 1)]
    span = tok_rows // PARTS

    hidden, fore, back = [], [None, []], [None, []]
    for start, count in ((0, span), (span, span)):
        gate_cut = gate_pre[start : start + count].astype(jnp.float32)
        up_cut = up_pre[start : start + count].astype(jnp.float32)
        hidden.append((gate_cut * jax.nn.sigmoid(gate_cut) * up_cut).astype(jnp.bfloat16))
        fore[1].append(lax.ppermute(hidden[-1].astype(wire), "row", ahead))
        back[1].append(lax.ppermute(hidden[-1].astype(wire), "row", behind))

    cot = spread_cotangent(grad_out, hidden, (fore[1][:1], back[1][:1]))
    turn = hidden[0]
    for step in range(2, rows + 1):
        fore.append([None] * PARTS)
        back.append([None] * PARTS)
        for at in range(PARTS):
            for ends, slot, mine, pairs in (
                (fore, rows + 1 - step, lambda row, step=step: step > row + 1, ahead),
                (back, step - 1, lambda row, step=step: step > rows - row, behind),
            ):
                sources = [
                    (after(piece, turn), first, count)
                    for piece, first, count in rows_of(ends[step - 1], at * span, span)
                ]
                turn = add_share(sources, cot, down_t, slot * tok_rows + at * span, mine)
                ends[step][at] = lax.ppermute(turn, "row", pairs)
        late = turn

    weight_grad = weight_product(cot, jnp.concatenate(hidden), fore[1:rows], back[1:rows], norm_scale)

    own_share = jnp.dot(after(cot[:tok_rows], late), down_t, preferred_element_type=jnp.float32)
    own_share, gate_again, up_again = after((own_share, gate_pre, up_pre), turn)
    grads = None
    for at in range(PARTS):
        grads = finish(gate_again, up_again, own_share, fore[rows][at], back[rows][at], at * span, grads)
    return *grads, weight_grad


def solution(mesh):
    specs = (P("row", "col"),) * 4
    return jax.shard_map(
        per_device, mesh=mesh, in_specs=specs, out_specs=specs[:3], check_vma=False
    )
```

```python
import jax
import jax.numpy as jnp
from jax import lax
from jax.experimental import pallas as pl
from jax.experimental.pallas import tpu as pltpu
from jax.sharding import PartitionSpec as P

PARTS = 2


def after(value, first):
    return lax.optimization_barrier((value, first))[0]


def lay_strips(near, far):
    chips = len(near)
    rows, strip, width = near[0].shape

    def kernel(*refs):
        row, col = lax.axis_index("row"), lax.axis_index("col")
        out_ref = refs[-1]
        for at, ref in enumerate(refs[:-1]):
            core, chip = at // chips, at % chips
            lane = pl.multiple_of(((col & 1) ^ core) * width, width)
            for group in range(rows):
                slot = lax.rem((row ^ group) + rows - row, rows)
                start = (slot * chips + (col // 2 ^ chip)) * strip
                out_ref[pl.ds(pl.multiple_of(start, strip), strip), pl.ds(lane, width)] = ref[group]

    return pl.pallas_call(
        kernel,
        out_shape=jax.ShapeDtypeStruct((rows * chips * strip, 2 * width), near[0].dtype),
        in_specs=[pl.BlockSpec(memory_space=pltpu.VMEM)] * 2 * chips,
        out_specs=pl.BlockSpec(memory_space=pltpu.VMEM),
        compiler_params=pltpu.CompilerParams(vmem_limit_bytes=32 * 2**20),
        name="lay_strips",
    )(*near, *far)


def add_share(sources, cot, down_t, start, mine):
    span = sum(count for _, _, count in sources)
    like = sources[0][0]
    width = like.shape[1]
    tile = 512 if width % 512 == 0 else width

    def kernel(*refs):
        got_refs, (cot_ref, down_ref, out_ref) = refs[: len(sources)], refs[len(sources) :]
        is_sum = mine(lax.axis_index("row"))
        places, at = [], 0
        for ref, (_, first, count) in zip(got_refs, sources):
            places.append((ref, slice(first, first + count), slice(at, at + count)))
            at += count

        @pl.when(is_sum)
        def _():
            tokens = cot_ref[start : start + span, :]
            for at in range(0, width, tile):
                cut = slice(at, at + tile)
                share = jnp.dot(tokens, down_ref[:, cut], preferred_element_type=jnp.float32)
                for ref, source, here in places:
                    total = ref[source, cut].astype(jnp.float32) + share[here]
                    out_ref[here, cut] = total.astype(out_ref.dtype)

        @pl.when(jnp.logical_not(is_sum))
        def _():
            for ref, source, here in places:
                out_ref[here, :] = ref[source, :]

    whole = pl.BlockSpec(memory_space=pltpu.VMEM)
    return pl.pallas_call(
        kernel,
        out_shape=jax.ShapeDtypeStruct((span, width), like.dtype),
        in_specs=[whole] * (2 + len(sources)),
        out_specs=whole,
        compiler_params=pltpu.CompilerParams(vmem_limit_bytes=32 * 2**20),
        cost_estimate=pl.CostEstimate(
            flops=2 * span * down_t.size, bytes_accessed=4 * span * width, transcendentals=0
        ),
        name="add_share",
    )(*(array for array, _, _ in sources), cot, down_t)


def rows_of(pieces, start, count):
    found, at = [], 0
    for piece in pieces:
        low, high = max(start, at), min(start + count, at + piece.shape[0])
        if low < high:
            found.append((piece, low - at, high - low))
        at += piece.shape[0]
    return found


def weight_product(cot, own, fore, back, scale):
    rows = len(fore) + 1
    tok_rows, width = own.shape
    tile = 512 if width % 512 == 0 else width
    flat = [piece for pieces in fore + back for piece in pieces]

    def kernel(cot_ref, own_ref, *refs):
        ends, (out_ref, hidden_ref) = iter(refs[: len(flat)]), refs[len(flat) :]
        fore_refs, back_refs = ([[next(ends) for _ in pieces] for pieces in way] for way in (fore, back))
        row = lax.axis_index("row")

        def place(pieces, start, cut):
            for piece in pieces:
                hidden_ref[start : start + piece.shape[0], :] = piece[:, cut].astype(hidden_ref.dtype)
                start += piece.shape[0]

        @pl.loop(0, width // tile)
        def _(at):
            cut = pl.ds(pl.multiple_of(at * tile, tile), tile)
            place([own_ref], 0, cut)
            for slot in range(1, rows):
                for here, pieces in (
                    (row + slot < rows, back_refs[slot - 1]),
                    (row + slot >= rows, fore_refs[rows - slot - 1]),
                ):
                    pl.when(here)(lambda pieces=pieces, slot=slot: place(pieces, slot * tok_rows, cut))
            total = lax.dot_general(
                cot_ref[...],
                hidden_ref[...],
                (((0,), (0,)), ((), ())),
                preferred_element_type=jnp.float32,
            )
            out_ref[:, cut] = (total * scale).astype(out_ref.dtype)

    whole = pl.BlockSpec(memory_space=pltpu.VMEM)
    return pl.pallas_call(
        kernel,
        out_shape=jax.ShapeDtypeStruct((cot.shape[1], width), jnp.bfloat16),
        in_specs=[whole] * (2 + len(flat)),
        out_specs=whole,
        scratch_shapes=[pltpu.VMEM((cot.shape[0], tile), jnp.bfloat16)],
        compiler_params=pltpu.CompilerParams(vmem_limit_bytes=32 * 2**20),
        cost_estimate=pl.CostEstimate(
            flops=2 * cot.size * width, bytes_accessed=4 * cot.shape[0] * width, transcendentals=0
        ),
        name="weight_product",
    )(cot, own, *flat)


def finish(gate_pre, up_pre, share, fore, back, start, grads):
    span, width = fore.shape
    tile = 512 if width % 512 == 0 else width
    old = () if grads is None else tuple(grads)

    def kernel(*refs):
        gate_ref, up_ref, share_ref, fore_ref, back_ref = refs[:5]
        outs, parts, sems = refs[5 + len(old) : 7 + len(old)], refs[-3:-1], refs[-1]
        here = slice(start, start + span)
        copies = []
        for at in range(0, width, tile):
            cut = slice(at, at + tile)
            grad = share_ref[here, cut] + fore_ref[:, cut].astype(jnp.float32) + back_ref[:, cut].astype(jnp.float32)
            gate = gate_ref[here, cut].astype(jnp.float32)
            sigmoid = jax.nn.sigmoid(gate)
            slope = sigmoid * (1.0 + gate * (1.0 - sigmoid))
            parts[0][:, cut] = (grad * up_ref[here, cut].astype(jnp.float32) * slope).astype(jnp.bfloat16)
            parts[1][:, cut] = (grad * (gate * sigmoid)).astype(jnp.bfloat16)
            for which, (part, out) in enumerate(zip(parts, outs)):
                copy = pltpu.make_async_copy(part.at[:, cut], out.at[here, cut], sems.at[which, at // tile])
                copy.start()
                copies.append(copy)
        for copy in copies:
            copy.wait()

    whole, anywhere = pl.BlockSpec(memory_space=pltpu.VMEM), pl.BlockSpec(memory_space=pl.ANY)
    return pl.pallas_call(
        kernel,
        out_shape=[jax.ShapeDtypeStruct(gate_pre.shape, jnp.bfloat16)] * 2,
        in_specs=[whole] * 5 + [anywhere] * len(old),
        out_specs=[anywhere] * 2,
        scratch_shapes=[pltpu.VMEM((span, width), jnp.bfloat16)] * 2
        + [pltpu.SemaphoreType.DMA((2, width // tile))],
        input_output_aliases={5 + at: at for at in range(len(old))},
        compiler_params=pltpu.CompilerParams(vmem_limit_bytes=32 * 2**20),
        cost_estimate=pl.CostEstimate(flops=20 * span * width, bytes_accessed=8 * span * width, transcendentals=span * width),
        name="finish",
    )(gate_pre, up_pre, share, fore, back, *old)


def swap(value, bits):
    return lax.ppermute(value, "col", [(at, at ^ bits) for at in range(lax.axis_size("col"))])


def spread_cotangent(grad_out, hidden, first):
    rows, cols = lax.axis_size("row"), lax.axis_size("col")
    row = lax.axis_index("row")
    tok_rows, width = grad_out.shape
    per_row = cols // rows
    if (rows, cols) != (4, 8):
        pairs = [
            (src * cols + per_row * dst + part, dst * cols + per_row * ((src - dst) % rows) + part)
            for src in range(rows)
            for dst in range(rows)
            for part in range(per_row)
        ]
        moved = lax.ppermute(grad_out, ("row", "col"), pairs)
        blocks = lax.all_gather(moved, "col", axis=0)
        blocks = blocks.reshape(rows, per_row, tok_rows, width)
        return blocks.transpose(0, 2, 1, 3).reshape(rows * tok_rows, per_row * width)
    strip = tok_rows * 2 // cols
    chip = lax.axis_index("col") // 2
    grad_out = after(grad_out, hidden[0])

    def quarter(bits):
        piece = lax.dynamic_slice_in_dim(grad_out, (chip ^ bits) * strip, strip, 0)
        return swap(piece, 2 * bits) if bits else piece

    wide = [quarter(bits) for bits in range(cols // 2)]

    def across(bits):
        piece = lax.dynamic_index_in_dim(jnp.stack(wide), chip ^ row ^ bits, 0, keepdims=False)
        return lax.ppermute(piece, "row", [(at, at ^ bits) for at in range(rows)]) if bits else piece

    tall = [across(bits) for bits in range(rows - 1, -1, -1)]
    tall = after(jnp.stack(tall[::-1]), first)
    near = [tall, swap(tall, 2), swap(tall, 4), swap(tall, 6)]
    return lay_strips(near, [swap(block, 1) for block in near])


def per_device(gate_pre, up_pre, down_t, grad_out):
    rows = lax.axis_size("row")
    row = lax.axis_index("row")
    tok_rows, width = gate_pre.shape
    norm_scale = (tok_rows * rows) ** (-0.5)
    wire = jnp.bfloat16 if rows <= 4 else jnp.float32
    ahead = [(at, at + 1) for at in range(rows - 1)]
    behind = [(at + 1, at) for at in range(rows - 1)]
    span = tok_rows // PARTS

    hidden, fore, back = [], [None, []], [None, []]
    for start, count in ((0, span), (span, span)):
        gate_cut = gate_pre[start : start + count].astype(jnp.float32)
        up_cut = up_pre[start : start + count].astype(jnp.float32)
        hidden.append((gate_cut * jax.nn.sigmoid(gate_cut) * up_cut).astype(jnp.bfloat16))
        fore[1].append(lax.ppermute(hidden[-1].astype(wire), "row", ahead))
        back[1].append(lax.ppermute(hidden[-1].astype(wire), "row", behind))

    cot = spread_cotangent(grad_out, hidden, (fore[1][:1], back[1][:1]))
    turn = hidden[0]
    for step in range(2, rows + 1):
        fore.append([None] * PARTS)
        back.append([None] * PARTS)
        for at in range(PARTS):
            for ends, slot, mine, pairs in (
                (fore, rows + 1 - step, lambda row, step=step: step > row + 1, ahead),
                (back, step - 1, lambda row, step=step: step > rows - row, behind),
            ):
                sources = [
                    (after(piece, turn), first, count)
                    for piece, first, count in rows_of(ends[step - 1], at * span, span)
                ]
                turn = add_share(sources, cot, down_t, slot * tok_rows + at * span, mine)
                ends[step][at] = lax.ppermute(turn, "row", pairs)
        late = turn

    weight_grad = weight_product(cot, jnp.concatenate(hidden), fore[1:rows], back[1:rows], norm_scale)

    own_share = jnp.dot(after(cot[:tok_rows], late), down_t, preferred_element_type=jnp.float32)
    own_share, gate_again, up_again = after((own_share, gate_pre, up_pre), turn)
    grads = None
    for at in range(PARTS):
        grads = finish(gate_again, up_again, own_share, fore[rows][at], back[rows][at], at * span, grads)
    return *grads, weight_grad


def solution(mesh):
    specs = (P("row", "col"),) * 4
    return jax.shard_map(
        per_device, mesh=mesh, in_specs=specs, out_specs=specs[:3], check_vma=False
    )
```

```python
import jax
import jax.numpy as jnp
from jax import lax
from jax.experimental import pallas as pl
from jax.experimental.pallas import tpu as pltpu
from jax.sharding import PartitionSpec as P

PARTS = 2


def after(value, first):
    return lax.optimization_barrier((value, first))[0]


def lay_strips(near, far):
    chips, rows, strip, width = near.shape

    def kernel(near_ref, *refs):
        row, col = lax.axis_index("row"), lax.axis_index("col")
        far_refs, out_ref = refs[:-1], refs[-1]
        for group in range(rows):
            slot = lax.rem((row ^ group) + rows - row, rows)
            for chip in range(chips):
                here = pl.ds(pl.multiple_of((slot * chips + chip) * strip, strip), strip)
                for core, strip_of in enumerate((near_ref[chip, group], far_refs[chip][group])):
                    lane = pl.multiple_of(((col & 1) ^ core) * width, width)
                    out_ref[here, pl.ds(lane, width)] = strip_of

    return pl.pallas_call(
        kernel,
        out_shape=jax.ShapeDtypeStruct((rows * chips * strip, 2 * width), near.dtype),
        in_specs=[pl.BlockSpec(memory_space=pltpu.VMEM)] * (1 + chips),
        out_specs=pl.BlockSpec(memory_space=pltpu.VMEM),
        compiler_params=pltpu.CompilerParams(vmem_limit_bytes=32 * 2**20),
        name="lay_strips",
    )(near, *far)


def add_share(sources, cot, down_t, start, mine):
    span = sum(count for _, _, count in sources)
    like = sources[0][0]
    width = like.shape[1]
    tile = 512 if width % 512 == 0 else width

    def kernel(*refs):
        got_refs, (cot_ref, down_ref, out_ref) = refs[: len(sources)], refs[len(sources) :]
        is_sum = mine(lax.axis_index("row"))
        places, at = [], 0
        for ref, (_, first, count) in zip(got_refs, sources):
            places.append((ref, slice(first, first + count), slice(at, at + count)))
            at += count

        @pl.when(is_sum)
        def _():
            tokens = cot_ref[start : start + span, :]
            for at in range(0, width, tile):
                cut = slice(at, at + tile)
                share = jnp.dot(tokens, down_ref[:, cut], preferred_element_type=jnp.float32)
                for ref, source, here in places:
                    total = ref[source, cut].astype(jnp.float32) + share[here]
                    out_ref[here, cut] = total.astype(out_ref.dtype)

        @pl.when(jnp.logical_not(is_sum))
        def _():
            for ref, source, here in places:
                out_ref[here, :] = ref[source, :]

    whole = pl.BlockSpec(memory_space=pltpu.VMEM)
    return pl.pallas_call(
        kernel,
        out_shape=jax.ShapeDtypeStruct((span, width), like.dtype),
        in_specs=[whole] * (2 + len(sources)),
        out_specs=whole,
        compiler_params=pltpu.CompilerParams(vmem_limit_bytes=32 * 2**20),
        cost_estimate=pl.CostEstimate(
            flops=2 * span * down_t.size, bytes_accessed=4 * span * width, transcendentals=0
        ),
        name="add_share",
    )(*(array for array, _, _ in sources), cot, down_t)


def rows_of(pieces, start, count):
    found, at = [], 0
    for piece in pieces:
        low, high = max(start, at), min(start + count, at + piece.shape[0])
        if low < high:
            found.append((piece, low - at, high - low))
        at += piece.shape[0]
    return found


def weight_product(cot, own, fore, back, scale):
    rows = len(fore) + 1
    tok_rows, width = own.shape
    tile = 512 if width % 512 == 0 else width
    flat = [piece for pieces in fore + back for piece in pieces]

    def kernel(cot_ref, own_ref, *refs):
        ends, (out_ref, hidden_ref) = iter(refs[: len(flat)]), refs[len(flat) :]
        fore_refs, back_refs = ([[next(ends) for _ in pieces] for pieces in way] for way in (fore, back))
        row = lax.axis_index("row")

        def place(pieces, start, cut):
            for piece in pieces:
                hidden_ref[start : start + piece.shape[0], :] = piece[:, cut].astype(hidden_ref.dtype)
                start += piece.shape[0]

        @pl.loop(0, width // tile)
        def _(at):
            cut = pl.ds(pl.multiple_of(at * tile, tile), tile)
            place([own_ref], 0, cut)
            for slot in range(1, rows):
                for here, pieces in (
                    (row + slot < rows, back_refs[slot - 1]),
                    (row + slot >= rows, fore_refs[rows - slot - 1]),
                ):
                    pl.when(here)(lambda pieces=pieces, slot=slot: place(pieces, slot * tok_rows, cut))
            total = lax.dot_general(
                cot_ref[...],
                hidden_ref[...],
                (((0,), (0,)), ((), ())),
                preferred_element_type=jnp.float32,
            )
            out_ref[:, cut] = (total * scale).astype(out_ref.dtype)

    whole = pl.BlockSpec(memory_space=pltpu.VMEM)
    return pl.pallas_call(
        kernel,
        out_shape=jax.ShapeDtypeStruct((cot.shape[1], width), jnp.bfloat16),
        in_specs=[whole] * (2 + len(flat)),
        out_specs=whole,
        scratch_shapes=[pltpu.VMEM((cot.shape[0], tile), jnp.bfloat16)],
        compiler_params=pltpu.CompilerParams(vmem_limit_bytes=32 * 2**20),
        cost_estimate=pl.CostEstimate(
            flops=2 * cot.size * width, bytes_accessed=4 * cot.shape[0] * width, transcendentals=0
        ),
        name="weight_product",
    )(cot, own, *flat)


def finish(gate_pre, up_pre, share, fore, back, start, grads):
    span, width = fore.shape
    tile = 512 if width % 512 == 0 else width
    old = () if grads is None else tuple(grads)

    def kernel(*refs):
        gate_ref, up_ref, share_ref, fore_ref, back_ref = refs[:5]
        outs, parts, sems = refs[5 + len(old) : 7 + len(old)], refs[-3:-1], refs[-1]
        here = slice(start, start + span)
        copies = []
        for at in range(0, width, tile):
            cut = slice(at, at + tile)
            grad = share_ref[here, cut] + fore_ref[:, cut].astype(jnp.float32) + back_ref[:, cut].astype(jnp.float32)
            gate = gate_ref[here, cut].astype(jnp.float32)
            sigmoid = jax.nn.sigmoid(gate)
            slope = sigmoid * (1.0 + gate * (1.0 - sigmoid))
            parts[0][:, cut] = (grad * up_ref[here, cut].astype(jnp.float32) * slope).astype(jnp.bfloat16)
            parts[1][:, cut] = (grad * (gate * sigmoid)).astype(jnp.bfloat16)
            for which, (part, out) in enumerate(zip(parts, outs)):
                copy = pltpu.make_async_copy(part.at[:, cut], out.at[here, cut], sems.at[which, at // tile])
                copy.start()
                copies.append(copy)
        for copy in copies:
            copy.wait()

    whole, anywhere = pl.BlockSpec(memory_space=pltpu.VMEM), pl.BlockSpec(memory_space=pl.ANY)
    return pl.pallas_call(
        kernel,
        out_shape=[jax.ShapeDtypeStruct(gate_pre.shape, jnp.bfloat16)] * 2,
        in_specs=[whole] * 5 + [anywhere] * len(old),
        out_specs=[anywhere] * 2,
        scratch_shapes=[pltpu.VMEM((span, width), jnp.bfloat16)] * 2
        + [pltpu.SemaphoreType.DMA((2, width // tile))],
        input_output_aliases={5 + at: at for at in range(len(old))},
        compiler_params=pltpu.CompilerParams(vmem_limit_bytes=32 * 2**20),
        cost_estimate=pl.CostEstimate(flops=20 * span * width, bytes_accessed=8 * span * width, transcendentals=span * width),
        name="finish",
    )(gate_pre, up_pre, share, fore, back, *old)


def swap(value, bits):
    return lax.ppermute(value, "col", [(at, at ^ bits) for at in range(lax.axis_size("col"))])


def spread_cotangent(grad_out, hidden, first, second):
    rows, cols = lax.axis_size("row"), lax.axis_size("col")
    row = lax.axis_index("row")
    tok_rows, width = grad_out.shape
    per_row = cols // rows
    if (rows, cols) != (4, 8):
        pairs = [
            (src * cols + per_row * dst + part, dst * cols + per_row * ((src - dst) % rows) + part)
            for src in range(rows)
            for dst in range(rows)
            for part in range(per_row)
        ]
        moved = lax.ppermute(grad_out, ("row", "col"), pairs)
        blocks = lax.all_gather(moved, "col", axis=0)
        blocks = blocks.reshape(rows, per_row, tok_rows, width)
        return blocks.transpose(0, 2, 1, 3).reshape(rows * tok_rows, per_row * width)
    strip = tok_rows * 2 // cols
    chip = lax.axis_index("col") // 2

    def quarter(bits):
        piece = lax.dynamic_slice_in_dim(grad_out, (chip ^ bits) * strip, strip, 0)
        return swap(piece, 2 * bits) if bits else piece

    wide = after([quarter(bits) for bits in range(cols // 2)], hidden[0])

    def across(bits):
        piece = lax.dynamic_index_in_dim(jnp.stack(wide), chip ^ row ^ bits, 0, keepdims=False)
        return lax.ppermute(piece, "row", [(at, at ^ bits) for at in range(rows)]) if bits else piece

    tall = [across(bits) for bits in range(rows - 1, -1, -1)]
    tall = jnp.stack(tall[::-1])
    same_core = [list(range(core, cols, 2)) for core in range(2)]
    near = lax.all_to_all(
        jnp.broadcast_to(tall, (cols // 2, *tall.shape)), "col", 0, 0, axis_index_groups=same_core
    )
    near = after(near, first)
    far = after([swap(near[at], 1) for at in range(cols // 2)], second)
    return lay_strips(near, far)


def per_device(gate_pre, up_pre, down_t, grad_out):
    rows = lax.axis_size("row")
    row = lax.axis_index("row")
    tok_rows, width = gate_pre.shape
    norm_scale = (tok_rows * rows) ** (-0.5)
    wire = jnp.bfloat16 if rows <= 4 else jnp.float32
    ahead = [(at, at + 1) for at in range(rows - 1)]
    behind = [(at + 1, at) for at in range(rows - 1)]
    span = tok_rows // PARTS

    hidden, fore, back = [], [None, []], [None, []]
    for start, count in ((0, span), (span, span)):
        gate_cut = gate_pre[start : start + count].astype(jnp.float32)
        up_cut = up_pre[start : start + count].astype(jnp.float32)
        hidden.append((gate_cut * jax.nn.sigmoid(gate_cut) * up_cut).astype(jnp.bfloat16))
        fore[1].append(lax.ppermute(hidden[-1].astype(wire), "row", ahead))
        back[1].append(lax.ppermute(hidden[-1].astype(wire), "row", behind))

    cot = spread_cotangent(grad_out, hidden, (fore[1][:1], back[1][:1]), (fore[1][1:], back[1][1:]))
    turn = hidden[0]
    for step in range(2, rows + 1):
        fore.append([None] * PARTS)
        back.append([None] * PARTS)
        for at in range(PARTS):
            for ends, slot, mine, pairs in (
                (fore, rows + 1 - step, lambda row, step=step: step > row + 1, ahead),
                (back, step - 1, lambda row, step=step: step > rows - row, behind),
            ):
                sources = [
                    (after(piece, turn), first, count)
                    for piece, first, count in rows_of(ends[step - 1], at * span, span)
                ]
                turn = add_share(sources, cot, down_t, slot * tok_rows + at * span, mine)
                ends[step][at] = lax.ppermute(turn, "row", pairs)
        late = turn

    weight_grad = weight_product(cot, jnp.concatenate(hidden), fore[1:rows], back[1:rows], norm_scale)

    own_share = jnp.dot(after(cot[:tok_rows], late), down_t, preferred_element_type=jnp.float32)
    own_share, gate_again, up_again = after((own_share, gate_pre, up_pre), turn)
    grads = None
    for at in range(PARTS):
        grads = finish(gate_again, up_again, own_share, fore[rows][at], back[rows][at], at * span, grads)
    return *grads, weight_grad


def solution(mesh):
    specs = (P("row", "col"),) * 4
    return jax.shard_map(
        per_device, mesh=mesh, in_specs=specs, out_specs=specs[:3], check_vma=False
    )
```

```python
import jax
import jax.numpy as jnp
from jax import lax
from jax.experimental import pallas as pl
from jax.experimental.pallas import tpu as pltpu
from jax.sharding import PartitionSpec as P


def after(value, first):
    return lax.optimization_barrier((value, first))[0]


def lay_strips(near, far):
    chips = len(near)
    rows, strip, width = near[0].shape

    def kernel(*refs):
        row, col = lax.axis_index("row"), lax.axis_index("col")
        out_ref = refs[-1]
        for at, ref in enumerate(refs[:-1]):
            core, chip = at // chips, at % chips
            lane = pl.multiple_of(((col & 1) ^ core) * width, width)
            for group in range(rows):
                slot = lax.rem((row ^ group) + rows - row, rows)
                start = (slot * chips + (col // 2 ^ chip)) * strip
                out_ref[pl.ds(pl.multiple_of(start, strip), strip), pl.ds(lane, width)] = ref[group]

    return pl.pallas_call(
        kernel,
        out_shape=jax.ShapeDtypeStruct((rows * chips * strip, 2 * width), near[0].dtype),
        in_specs=[pl.BlockSpec(memory_space=pltpu.VMEM)] * 2 * chips,
        out_specs=pl.BlockSpec(memory_space=pltpu.VMEM),
        compiler_params=pltpu.CompilerParams(vmem_limit_bytes=32 * 2**20),
        name="lay_strips",
    )(*near, *far)


def goes_ahead(way):
    return (lax.axis_index("col") & 1) == way


def ring(value, way):
    rows, cols = lax.axis_size("row"), lax.axis_size("col")
    pairs = []
    for row in range(rows):
        for col in range(cols):
            to = row + 1 if col & 1 == way else row - 1
            if 0 <= to < rows:
                pairs.append((row * cols + col, to * cols + col))
    return lax.ppermute(value, ("row", "col"), pairs)


def add_share(got, cot, down_t, way, step, first, tok_rows):
    span, width = got.shape
    tile = 512 if width % 512 == 0 else width

    def kernel(got_ref, cot_ref, down_ref, out_ref):
        rows, row, ahead = lax.axis_size("row"), lax.axis_index("row"), goes_ahead(way)
        is_sum = step > jnp.where(ahead, row + 1, rows - row)
        start = jnp.where(ahead, rows + 1 - step, step - 1) * tok_rows + first

        @pl.when(is_sum)
        def _():
            tokens = cot_ref[pl.ds(pl.multiple_of(start, 16), span), :]
            for at in range(0, width, tile):
                cut = slice(at, at + tile)
                share = jnp.dot(tokens, down_ref[:, cut], preferred_element_type=jnp.float32)
                out_ref[:, cut] = (got_ref[:, cut].astype(jnp.float32) + share).astype(out_ref.dtype)

        @pl.when(jnp.logical_not(is_sum))
        def _():
            out_ref[...] = got_ref[...]

    whole = pl.BlockSpec(memory_space=pltpu.VMEM)
    return pl.pallas_call(
        kernel,
        out_shape=jax.ShapeDtypeStruct(got.shape, got.dtype),
        in_specs=[whole] * 3,
        out_specs=whole,
        compiler_params=pltpu.CompilerParams(vmem_limit_bytes=32 * 2**20),
        cost_estimate=pl.CostEstimate(
            flops=2 * span * down_t.size, bytes_accessed=4 * span * width, transcendentals=0
        ),
        name="add_share",
    )(got, cot, down_t)


def weight_product(cot, own, ways, scale):
    rows = len(ways[0]) + 1
    tok_rows, width = own.shape
    tile = 512 if width % 512 == 0 else width
    flat = [piece for steps in ways for pieces in steps for piece in pieces]

    def kernel(cot_ref, own_ref, *refs):
        ends, (out_ref, hidden_ref) = iter(refs[: len(flat)]), refs[len(flat) :]
        way_refs = [[[next(ends) for _ in pieces] for pieces in steps] for steps in ways]
        row = lax.axis_index("row")

        def place(pieces, start, cut):
            for piece in pieces:
                hidden_ref[start : start + piece.shape[0], :] = piece[:, cut].astype(hidden_ref.dtype)
                start += piece.shape[0]

        @pl.loop(0, width // tile)
        def _(at):
            cut = pl.ds(pl.multiple_of(at * tile, tile), tile)
            place([own_ref], 0, cut)
            for slot in range(1, rows):
                for way, refs_of in enumerate(way_refs):
                    ahead, from_next = goes_ahead(way), row + slot < rows
                    for here, step in (
                        (jnp.logical_and(from_next, jnp.logical_not(ahead)), slot),
                        (jnp.logical_and(jnp.logical_not(from_next), ahead), rows - slot),
                    ):
                        pieces = refs_of[step - 1]
                        pl.when(here)(lambda pieces=pieces, slot=slot: place(pieces, slot * tok_rows, cut))
            total = lax.dot_general(
                cot_ref[...],
                hidden_ref[...],
                (((0,), (0,)), ((), ())),
                preferred_element_type=jnp.float32,
            )
            out_ref[:, cut] = (total * scale).astype(out_ref.dtype)

    whole = pl.BlockSpec(memory_space=pltpu.VMEM)
    return pl.pallas_call(
        kernel,
        out_shape=jax.ShapeDtypeStruct((cot.shape[1], width), jnp.bfloat16),
        in_specs=[whole] * (2 + len(flat)),
        out_specs=whole,
        scratch_shapes=[pltpu.VMEM((cot.shape[0], tile), jnp.bfloat16)],
        compiler_params=pltpu.CompilerParams(vmem_limit_bytes=32 * 2**20),
        cost_estimate=pl.CostEstimate(
            flops=2 * cot.size * width, bytes_accessed=4 * cot.shape[0] * width, transcendentals=0
        ),
        name="weight_product",
    )(cot, own, *flat)


def finish(gate_pre, up_pre, share, fore, back, start, grads):
    span, width = fore.shape
    tile = 512 if width % 512 == 0 else width
    old = () if grads is None else tuple(grads)

    def kernel(*refs):
        gate_ref, up_ref, share_ref, fore_ref, back_ref = refs[:5]
        outs, parts, sems = refs[5 + len(old) : 7 + len(old)], refs[-3:-1], refs[-1]
        here = slice(start, start + span)
        copies = []
        for at in range(0, width, tile):
            cut = slice(at, at + tile)
            grad = share_ref[here, cut] + fore_ref[:, cut].astype(jnp.float32) + back_ref[:, cut].astype(jnp.float32)
            gate = gate_ref[here, cut].astype(jnp.float32)
            sigmoid = jax.nn.sigmoid(gate)
            slope = sigmoid * (1.0 + gate * (1.0 - sigmoid))
            parts[0][:, cut] = (grad * up_ref[here, cut].astype(jnp.float32) * slope).astype(jnp.bfloat16)
            parts[1][:, cut] = (grad * (gate * sigmoid)).astype(jnp.bfloat16)
            for which, (part, out) in enumerate(zip(parts, outs)):
                copy = pltpu.make_async_copy(part.at[:, cut], out.at[here, cut], sems.at[which, at // tile])
                copy.start()
                copies.append(copy)
        for copy in copies:
            copy.wait()

    whole, anywhere = pl.BlockSpec(memory_space=pltpu.VMEM), pl.BlockSpec(memory_space=pl.ANY)
    return pl.pallas_call(
        kernel,
        out_shape=[jax.ShapeDtypeStruct(gate_pre.shape, jnp.bfloat16)] * 2,
        in_specs=[whole] * 5 + [anywhere] * len(old),
        out_specs=[anywhere] * 2,
        scratch_shapes=[pltpu.VMEM((span, width), jnp.bfloat16)] * 2
        + [pltpu.SemaphoreType.DMA((2, width // tile))],
        input_output_aliases={5 + at: at for at in range(len(old))},
        compiler_params=pltpu.CompilerParams(vmem_limit_bytes=32 * 2**20),
        cost_estimate=pl.CostEstimate(flops=20 * span * width, bytes_accessed=8 * span * width, transcendentals=span * width),
        name="finish",
    )(gate_pre, up_pre, share, fore, back, *old)


def swap(value, bits):
    return lax.ppermute(value, "col", [(at, at ^ bits) for at in range(lax.axis_size("col"))])


def spread_cotangent(grad_out, hidden, first):
    rows, cols = lax.axis_size("row"), lax.axis_size("col")
    row = lax.axis_index("row")
    tok_rows, width = grad_out.shape
    per_row = cols // rows
    if (rows, cols) != (4, 8):
        pairs = [
            (src * cols + per_row * dst + part, dst * cols + per_row * ((src - dst) % rows) + part)
            for src in range(rows)
            for dst in range(rows)
            for part in range(per_row)
        ]
        moved = lax.ppermute(grad_out, ("row", "col"), pairs)
        blocks = lax.all_gather(moved, "col", axis=0)
        blocks = blocks.reshape(rows, per_row, tok_rows, width)
        return blocks.transpose(0, 2, 1, 3).reshape(rows * tok_rows, per_row * width)
    strip = tok_rows * 2 // cols
    chip = lax.axis_index("col") // 2

    def quarter(bits):
        piece = lax.dynamic_slice_in_dim(grad_out, (chip ^ bits) * strip, strip, 0)
        return swap(piece, 2 * bits) if bits else piece

    wide = after([quarter(bits) for bits in range(cols // 2)], hidden[0])

    def across(bits):
        piece = lax.dynamic_index_in_dim(jnp.stack(wide), chip ^ row ^ bits, 0, keepdims=False)
        return lax.ppermute(piece, "row", [(at, at ^ bits) for at in range(rows)]) if bits else piece

    tall = [across(bits) for bits in range(rows - 1, -1, -1)]
    tall = jnp.stack(tall[::-1])
    near = [tall, swap(tall, 2), swap(tall, 4), swap(tall, 6)]
    near[-1] = after(near[-1], first)
    far = [swap(block, 1) for block in near]
    return lay_strips(near, far)


def per_device(gate_pre, up_pre, down_t, grad_out):
    rows = lax.axis_size("row")
    tok_rows, width = gate_pre.shape
    norm_scale = (tok_rows * rows) ** (-0.5)
    wire = jnp.bfloat16 if rows <= 4 else jnp.float32
    lead = tok_rows * 8 // 16
    chains = ((0, lead), (lead, tok_rows - lead))

    hidden, ways = [], ([[]], [[]])
    for start, count in chains:
        gate_cut = gate_pre[start : start + count].astype(jnp.float32)
        up_cut = up_pre[start : start + count].astype(jnp.float32)
        hidden.append((gate_cut * jax.nn.sigmoid(gate_cut) * up_cut).astype(jnp.bfloat16))
        for way, steps in enumerate(ways):
            steps[0].append(ring(hidden[-1].astype(wire), way))

    cot = spread_cotangent(grad_out, hidden, [steps[0][0] for steps in ways])
    turn = hidden[0]
    for step in range(2, rows + 1):
        for steps in ways:
            steps.append([])
        for at, (first, _) in enumerate(chains):
            for way, steps in enumerate(ways):
                got = after(steps[-2][at], turn)
                turn = add_share(got, cot, down_t, way, step, first, tok_rows)
                steps[-1].append(ring(turn, way))
        late = turn

    weight_grad = weight_product(cot, jnp.concatenate(hidden), [steps[:-1] for steps in ways], norm_scale)

    own_share = jnp.dot(after(cot[:tok_rows], late), down_t, preferred_element_type=jnp.float32)
    own_share, gate_again, up_again = after((own_share, gate_pre, up_pre), turn)
    grads = None
    for at, (first, _) in enumerate(chains):
        grads = finish(gate_again, up_again, own_share, ways[0][-1][at], ways[1][-1][at], first, grads)
    return *grads, weight_grad


def solution(mesh):
    specs = (P("row", "col"),) * 4
    return jax.shard_map(
        per_device, mesh=mesh, in_specs=specs, out_specs=specs[:3], check_vma=False
    )
```

```python
import jax
import jax.numpy as jnp
from jax import lax
from jax.experimental import pallas as pl
from jax.experimental.pallas import tpu as pltpu
from jax.sharding import PartitionSpec as P


def after(value, first):
    return lax.optimization_barrier((value, first))[0]


def lay_strips(near, far):
    chips = len(near)
    rows, strip, width = near[0].shape

    def kernel(*refs):
        row, col = lax.axis_index("row"), lax.axis_index("col")
        out_ref = refs[-1]
        for at, ref in enumerate(refs[:-1]):
            core, chip = at // chips, at % chips
            lane = pl.multiple_of(((col & 1) ^ core) * width, width)
            for group in range(rows):
                slot = lax.rem((row ^ group) + rows - row, rows)
                start = (slot * chips + (col // 2 ^ chip)) * strip
                out_ref[pl.ds(pl.multiple_of(start, strip), strip), pl.ds(lane, width)] = ref[group]

    return pl.pallas_call(
        kernel,
        out_shape=jax.ShapeDtypeStruct((rows * chips * strip, 2 * width), near[0].dtype),
        in_specs=[pl.BlockSpec(memory_space=pltpu.VMEM)] * 2 * chips,
        out_specs=pl.BlockSpec(memory_space=pltpu.VMEM),
        compiler_params=pltpu.CompilerParams(vmem_limit_bytes=32 * 2**20),
        name="lay_strips",
    )(*near, *far)


def goes_ahead(way):
    return (lax.axis_index("col") & 1) == way


def ring(value, way):
    rows, cols = lax.axis_size("row"), lax.axis_size("col")
    pairs = []
    for row in range(rows):
        for col in range(cols):
            to = row + 1 if col & 1 == way else row - 1
            if 0 <= to < rows:
                pairs.append((row * cols + col, to * cols + col))
    return lax.ppermute(value, ("row", "col"), pairs)


def add_share(got, cot, down_t, way, step, first, tok_rows):
    span, width = got.shape
    tile = 512 if width % 512 == 0 else width

    def kernel(got_ref, cot_ref, down_ref, out_ref):
        rows, row, ahead = lax.axis_size("row"), lax.axis_index("row"), goes_ahead(way)
        is_sum = step > jnp.where(ahead, row + 1, rows - row)
        start = jnp.where(ahead, rows + 1 - step, step - 1) * tok_rows + first

        @pl.when(is_sum)
        def _():
            tokens = cot_ref[pl.ds(pl.multiple_of(start, 16), span), :]
            for at in range(0, width, tile):
                cut = slice(at, at + tile)
                share = jnp.dot(tokens, down_ref[:, cut], preferred_element_type=jnp.float32)
                out_ref[:, cut] = (got_ref[:, cut].astype(jnp.float32) + share).astype(out_ref.dtype)

        @pl.when(jnp.logical_not(is_sum))
        def _():
            out_ref[...] = got_ref[...]

    whole = pl.BlockSpec(memory_space=pltpu.VMEM)
    return pl.pallas_call(
        kernel,
        out_shape=jax.ShapeDtypeStruct(got.shape, got.dtype),
        in_specs=[whole] * 3,
        out_specs=whole,
        compiler_params=pltpu.CompilerParams(vmem_limit_bytes=32 * 2**20),
        cost_estimate=pl.CostEstimate(
            flops=2 * span * down_t.size, bytes_accessed=4 * span * width, transcendentals=0
        ),
        name="add_share",
    )(got, cot, down_t)


def weight_product(cot, own, ways, scale):
    rows = len(ways[0]) + 1
    tok_rows, width = own.shape
    tile = 512 if width % 512 == 0 else width
    flat = [piece for steps in ways for pieces in steps for piece in pieces]

    def kernel(cot_ref, own_ref, *refs):
        ends, (out_ref, hidden_ref) = iter(refs[: len(flat)]), refs[len(flat) :]
        way_refs = [[[next(ends) for _ in pieces] for pieces in steps] for steps in ways]
        row = lax.axis_index("row")

        def place(pieces, start, cut):
            for piece in pieces:
                hidden_ref[start : start + piece.shape[0], :] = piece[:, cut].astype(hidden_ref.dtype)
                start += piece.shape[0]

        @pl.loop(0, width // tile)
        def _(at):
            cut = pl.ds(pl.multiple_of(at * tile, tile), tile)
            place([own_ref], 0, cut)
            for slot in range(1, rows):
                for way, refs_of in enumerate(way_refs):
                    ahead, from_next = goes_ahead(way), row + slot < rows
                    for here, step in (
                        (jnp.logical_and(from_next, jnp.logical_not(ahead)), slot),
                        (jnp.logical_and(jnp.logical_not(from_next), ahead), rows - slot),
                    ):
                        pieces = refs_of[step - 1]
                        pl.when(here)(lambda pieces=pieces, slot=slot: place(pieces, slot * tok_rows, cut))
            total = lax.dot_general(
                cot_ref[...],
                hidden_ref[...],
                (((0,), (0,)), ((), ())),
                preferred_element_type=jnp.float32,
            )
            out_ref[:, cut] = (total * scale).astype(out_ref.dtype)

    whole = pl.BlockSpec(memory_space=pltpu.VMEM)
    return pl.pallas_call(
        kernel,
        out_shape=jax.ShapeDtypeStruct((cot.shape[1], width), jnp.bfloat16),
        in_specs=[whole] * (2 + len(flat)),
        out_specs=whole,
        scratch_shapes=[pltpu.VMEM((cot.shape[0], tile), jnp.bfloat16)],
        compiler_params=pltpu.CompilerParams(vmem_limit_bytes=32 * 2**20),
        cost_estimate=pl.CostEstimate(
            flops=2 * cot.size * width, bytes_accessed=4 * cot.shape[0] * width, transcendentals=0
        ),
        name="weight_product",
    )(cot, own, *flat)


def finish(gate_pre, up_pre, share, fore, back, start, grads):
    span, width = fore.shape
    tile = 512 if width % 512 == 0 else width
    old = () if grads is None else tuple(grads)

    def kernel(*refs):
        gate_ref, up_ref, share_ref, fore_ref, back_ref = refs[:5]
        outs, parts, sems = refs[5 + len(old) : 7 + len(old)], refs[-3:-1], refs[-1]
        here = slice(start, start + span)
        copies = []
        for at in range(0, width, tile):
            cut = slice(at, at + tile)
            grad = share_ref[here, cut] + fore_ref[:, cut].astype(jnp.float32) + back_ref[:, cut].astype(jnp.float32)
            gate = gate_ref[here, cut].astype(jnp.float32)
            sigmoid = jax.nn.sigmoid(gate)
            slope = sigmoid * (1.0 + gate * (1.0 - sigmoid))
            parts[0][:, cut] = (grad * up_ref[here, cut].astype(jnp.float32) * slope).astype(jnp.bfloat16)
            parts[1][:, cut] = (grad * (gate * sigmoid)).astype(jnp.bfloat16)
            for which, (part, out) in enumerate(zip(parts, outs)):
                copy = pltpu.make_async_copy(part.at[:, cut], out.at[here, cut], sems.at[which, at // tile])
                copy.start()
                copies.append(copy)
        for copy in copies:
            copy.wait()

    whole, anywhere = pl.BlockSpec(memory_space=pltpu.VMEM), pl.BlockSpec(memory_space=pl.ANY)
    return pl.pallas_call(
        kernel,
        out_shape=[jax.ShapeDtypeStruct(gate_pre.shape, jnp.bfloat16)] * 2,
        in_specs=[whole] * 5 + [anywhere] * len(old),
        out_specs=[anywhere] * 2,
        scratch_shapes=[pltpu.VMEM((span, width), jnp.bfloat16)] * 2
        + [pltpu.SemaphoreType.DMA((2, width // tile))],
        input_output_aliases={5 + at: at for at in range(len(old))},
        compiler_params=pltpu.CompilerParams(vmem_limit_bytes=32 * 2**20),
        cost_estimate=pl.CostEstimate(flops=20 * span * width, bytes_accessed=8 * span * width, transcendentals=span * width),
        name="finish",
    )(gate_pre, up_pre, share, fore, back, *old)


def swap(value, bits):
    return lax.ppermute(value, "col", [(at, at ^ bits) for at in range(lax.axis_size("col"))])


def spread_cotangent(grad_out, hidden, first, second):
    rows, cols = lax.axis_size("row"), lax.axis_size("col")
    row = lax.axis_index("row")
    tok_rows, width = grad_out.shape
    per_row = cols // rows
    if (rows, cols) != (4, 8):
        pairs = [
            (src * cols + per_row * dst + part, dst * cols + per_row * ((src - dst) % rows) + part)
            for src in range(rows)
            for dst in range(rows)
            for part in range(per_row)
        ]
        moved = lax.ppermute(grad_out, ("row", "col"), pairs)
        blocks = lax.all_gather(moved, "col", axis=0)
        blocks = blocks.reshape(rows, per_row, tok_rows, width)
        return blocks.transpose(0, 2, 1, 3).reshape(rows * tok_rows, per_row * width)
    strip = tok_rows * 2 // cols
    chip = lax.axis_index("col") // 2

    def quarter(bits):
        piece = lax.dynamic_slice_in_dim(grad_out, (chip ^ bits) * strip, strip, 0)
        return swap(piece, 2 * bits) if bits else piece

    wide = after([quarter(bits) for bits in range(cols // 2)], hidden[0])

    def across(bits):
        piece = lax.dynamic_index_in_dim(jnp.stack(wide), chip ^ row ^ bits, 0, keepdims=False)
        return lax.ppermute(piece, "row", [(at, at ^ bits) for at in range(rows)]) if bits else piece

    tall = [across(bits) for bits in range(rows - 1, -1, -1)]
    tall = jnp.stack(tall[::-1])
    near = [tall, swap(tall, 2), swap(tall, 4), swap(tall, 6)]
    near[3] = after(near[3], first)
    far = [swap(block, 1) for block in near]
    far = after(far, second)
    return lay_strips(near, far)


def per_device(gate_pre, up_pre, down_t, grad_out):
    rows = lax.axis_size("row")
    tok_rows, width = gate_pre.shape
    norm_scale = (tok_rows * rows) ** (-0.5)
    wire = jnp.bfloat16 if rows <= 4 else jnp.float32
    lead = tok_rows * 8 // 16
    chains = ((0, lead), (lead, tok_rows - lead))

    hidden, ways = [], ([[]], [[]])
    for start, count in chains:
        gate_cut = gate_pre[start : start + count].astype(jnp.float32)
        up_cut = up_pre[start : start + count].astype(jnp.float32)
        hidden.append((gate_cut * jax.nn.sigmoid(gate_cut) * up_cut).astype(jnp.bfloat16))
        for way, steps in enumerate(ways):
            steps[0].append(ring(hidden[-1].astype(wire), way))

    cot = spread_cotangent(grad_out, hidden, [steps[0][0] for steps in ways], [steps[0][1] for steps in ways])
    turn = hidden[0]
    for step in range(2, rows + 1):
        for steps in ways:
            steps.append([])
        for at, (first, _) in enumerate(chains):
            for way, steps in enumerate(ways):
                got = after(steps[-2][at], turn)
                turn = add_share(got, cot, down_t, way, step, first, tok_rows)
                steps[-1].append(ring(turn, way))
        late = turn

    weight_grad = weight_product(cot, jnp.concatenate(hidden), [steps[:-1] for steps in ways], norm_scale)

    own_share = jnp.dot(after(cot[:tok_rows], late), down_t, preferred_element_type=jnp.float32)
    own_share, gate_again, up_again = after((own_share, gate_pre, up_pre), turn)
    grads = None
    for at, (first, _) in enumerate(chains):
        grads = finish(gate_again, up_again, own_share, ways[0][-1][at], ways[1][-1][at], first, grads)
    return *grads, weight_grad


def solution(mesh):
    specs = (P("row", "col"),) * 4
    return jax.shard_map(
        per_device, mesh=mesh, in_specs=specs, out_specs=specs[:3], check_vma=False
    )
```

```python
import jax
import jax.numpy as jnp
from jax import lax
from jax.experimental import pallas as pl
from jax.experimental.pallas import tpu as pltpu
from jax.sharding import PartitionSpec as P


def after(value, first):
    return lax.optimization_barrier((value, first))[0]


def lay_strips(near, far):
    chips = len(near)
    rows, strip, width = near[0].shape

    def kernel(*refs):
        row, col = lax.axis_index("row"), lax.axis_index("col")
        out_ref = refs[-1]
        for at, ref in enumerate(refs[:-1]):
            core, chip = at // chips, at % chips
            lane = pl.multiple_of(((col & 1) ^ core) * width, width)
            for group in range(rows):
                slot = lax.rem((row ^ group) + rows - row, rows)
                start = (slot * chips + (col // 2 ^ chip)) * strip
                out_ref[pl.ds(pl.multiple_of(start, strip), strip), pl.ds(lane, width)] = ref[group]

    return pl.pallas_call(
        kernel,
        out_shape=jax.ShapeDtypeStruct((rows * chips * strip, 2 * width), near[0].dtype),
        in_specs=[pl.BlockSpec(memory_space=pltpu.VMEM)] * 2 * chips,
        out_specs=pl.BlockSpec(memory_space=pltpu.VMEM),
        compiler_params=pltpu.CompilerParams(vmem_limit_bytes=32 * 2**20),
        name="lay_strips",
    )(*near, *far)


def goes_ahead(way):
    return (lax.axis_index("col") & 1) == way


def ring(value, way):
    rows, cols = lax.axis_size("row"), lax.axis_size("col")
    pairs = []
    for row in range(rows):
        for col in range(cols):
            to = row + 1 if col & 1 == way else row - 1
            if 0 <= to < rows:
                pairs.append((row * cols + col, to * cols + col))
    return lax.ppermute(value, ("row", "col"), pairs)


def add_share(got, cot, down_t, way, step, first, tok_rows):
    span, width = got.shape
    tile = 512 if width % 512 == 0 else width

    def kernel(got_ref, cot_ref, down_ref, out_ref):
        rows, row, ahead = lax.axis_size("row"), lax.axis_index("row"), goes_ahead(way)
        is_sum = step > jnp.where(ahead, row + 1, rows - row)
        start = jnp.where(ahead, rows + 1 - step, step - 1) * tok_rows + first

        @pl.when(is_sum)
        def _():
            tokens = cot_ref[pl.ds(pl.multiple_of(start, 16), span), :]
            for at in range(0, width, tile):
                cut = slice(at, at + tile)
                share = jnp.dot(tokens, down_ref[:, cut], preferred_element_type=jnp.float32)
                out_ref[:, cut] = (got_ref[:, cut].astype(jnp.float32) + share).astype(out_ref.dtype)

        @pl.when(jnp.logical_not(is_sum))
        def _():
            out_ref[...] = got_ref[...]

    whole = pl.BlockSpec(memory_space=pltpu.VMEM)
    return pl.pallas_call(
        kernel,
        out_shape=jax.ShapeDtypeStruct(got.shape, got.dtype),
        in_specs=[whole] * 3,
        out_specs=whole,
        compiler_params=pltpu.CompilerParams(vmem_limit_bytes=32 * 2**20),
        cost_estimate=pl.CostEstimate(
            flops=2 * span * down_t.size, bytes_accessed=4 * span * width, transcendentals=0
        ),
        name="add_share",
    )(got, cot, down_t)


def weight_product(cot, own, ways, scale):
    rows = len(ways[0]) + 1
    tok_rows, width = own.shape
    tile = 512 if width % 512 == 0 else width
    flat = [piece for steps in ways for pieces in steps for piece in pieces]

    def kernel(cot_ref, own_ref, *refs):
        ends, (out_ref, hidden_ref) = iter(refs[: len(flat)]), refs[len(flat) :]
        way_refs = [[[next(ends) for _ in pieces] for pieces in steps] for steps in ways]
        row = lax.axis_index("row")

        def place(pieces, start, cut):
            for piece in pieces:
                hidden_ref[start : start + piece.shape[0], :] = piece[:, cut].astype(hidden_ref.dtype)
                start += piece.shape[0]

        @pl.loop(0, width // tile)
        def _(at):
            cut = pl.ds(pl.multiple_of(at * tile, tile), tile)
            place([own_ref], 0, cut)
            for slot in range(1, rows):
                for way, refs_of in enumerate(way_refs):
                    ahead, from_next = goes_ahead(way), row + slot < rows
                    for here, step in (
                        (jnp.logical_and(from_next, jnp.logical_not(ahead)), slot),
                        (jnp.logical_and(jnp.logical_not(from_next), ahead), rows - slot),
                    ):
                        pieces = refs_of[step - 1]
                        pl.when(here)(lambda pieces=pieces, slot=slot: place(pieces, slot * tok_rows, cut))
            total = lax.dot_general(
                cot_ref[...],
                hidden_ref[...],
                (((0,), (0,)), ((), ())),
                preferred_element_type=jnp.float32,
            )
            out_ref[:, cut] = (total * scale).astype(out_ref.dtype)

    whole = pl.BlockSpec(memory_space=pltpu.VMEM)
    return pl.pallas_call(
        kernel,
        out_shape=jax.ShapeDtypeStruct((cot.shape[1], width), jnp.bfloat16),
        in_specs=[whole] * (2 + len(flat)),
        out_specs=whole,
        scratch_shapes=[pltpu.VMEM((cot.shape[0], tile), jnp.bfloat16)],
        compiler_params=pltpu.CompilerParams(vmem_limit_bytes=32 * 2**20),
        cost_estimate=pl.CostEstimate(
            flops=2 * cot.size * width, bytes_accessed=4 * cot.shape[0] * width, transcendentals=0
        ),
        name="weight_product",
    )(cot, own, *flat)


def finish(gate_pre, up_pre, share, fore, back, start, grads):
    span, width = fore.shape
    tile = 512 if width % 512 == 0 else width
    old = () if grads is None else tuple(grads)

    def kernel(*refs):
        gate_ref, up_ref, share_ref, fore_ref, back_ref = refs[:5]
        outs, parts, sems = refs[5 + len(old) : 7 + len(old)], refs[-3:-1], refs[-1]
        here = slice(start, start + span)
        copies = []
        for at in range(0, width, tile):
            cut = slice(at, at + tile)
            grad = share_ref[here, cut] + fore_ref[:, cut].astype(jnp.float32) + back_ref[:, cut].astype(jnp.float32)
            gate = gate_ref[here, cut].astype(jnp.float32)
            sigmoid = jax.nn.sigmoid(gate)
            slope = sigmoid * (1.0 + gate * (1.0 - sigmoid))
            parts[0][:, cut] = (grad * up_ref[here, cut].astype(jnp.float32) * slope).astype(jnp.bfloat16)
            parts[1][:, cut] = (grad * (gate * sigmoid)).astype(jnp.bfloat16)
            for which, (part, out) in enumerate(zip(parts, outs)):
                copy = pltpu.make_async_copy(part.at[:, cut], out.at[here, cut], sems.at[which, at // tile])
                copy.start()
                copies.append(copy)
        for copy in copies:
            copy.wait()

    whole, anywhere = pl.BlockSpec(memory_space=pltpu.VMEM), pl.BlockSpec(memory_space=pl.ANY)
    return pl.pallas_call(
        kernel,
        out_shape=[jax.ShapeDtypeStruct(gate_pre.shape, jnp.bfloat16)] * 2,
        in_specs=[whole] * 5 + [anywhere] * len(old),
        out_specs=[anywhere] * 2,
        scratch_shapes=[pltpu.VMEM((span, width), jnp.bfloat16)] * 2
        + [pltpu.SemaphoreType.DMA((2, width // tile))],
        input_output_aliases={5 + at: at for at in range(len(old))},
        compiler_params=pltpu.CompilerParams(vmem_limit_bytes=32 * 2**20),
        cost_estimate=pl.CostEstimate(flops=20 * span * width, bytes_accessed=8 * span * width, transcendentals=span * width),
        name="finish",
    )(gate_pre, up_pre, share, fore, back, *old)


def swap(value, bits):
    return lax.ppermute(value, "col", [(at, at ^ bits) for at in range(lax.axis_size("col"))])


def spread_cotangent(grad_out, hidden, first, second):
    rows, cols = lax.axis_size("row"), lax.axis_size("col")
    row = lax.axis_index("row")
    tok_rows, width = grad_out.shape
    per_row = cols // rows
    if (rows, cols) != (4, 8):
        pairs = [
            (src * cols + per_row * dst + part, dst * cols + per_row * ((src - dst) % rows) + part)
            for src in range(rows)
            for dst in range(rows)
            for part in range(per_row)
        ]
        moved = lax.ppermute(grad_out, ("row", "col"), pairs)
        blocks = lax.all_gather(moved, "col", axis=0)
        blocks = blocks.reshape(rows, per_row, tok_rows, width)
        return blocks.transpose(0, 2, 1, 3).reshape(rows * tok_rows, per_row * width)
    strip = tok_rows * 2 // cols
    chip = lax.axis_index("col") // 2

    def quarter(bits):
        piece = lax.dynamic_slice_in_dim(grad_out, (chip ^ bits) * strip, strip, 0)
        return swap(piece, 2 * bits) if bits else piece

    wide = after([quarter(bits) for bits in range(cols // 2)], hidden[0])

    def across(bits):
        piece = lax.dynamic_index_in_dim(jnp.stack(wide), chip ^ row ^ bits, 0, keepdims=False)
        return lax.ppermute(piece, "row", [(at, at ^ bits) for at in range(rows)]) if bits else piece

    tall = [across(bits) for bits in range(rows - 1, -1, -1)]
    tall = jnp.stack(tall[::-1])
    near = [tall, swap(tall, 2), swap(tall, 4), swap(tall, 6)]
    near[3] = after(near[3], first)
    far = [swap(block, 1) for block in near]
    far = after(far, second[0])
    return lay_strips(near, far)


def per_device(gate_pre, up_pre, down_t, grad_out):
    rows = lax.axis_size("row")
    tok_rows, width = gate_pre.shape
    norm_scale = (tok_rows * rows) ** (-0.5)
    wire = jnp.bfloat16 if rows <= 4 else jnp.float32
    lead = tok_rows * 8 // 16
    chains = ((0, lead), (lead, tok_rows - lead))

    hidden, ways = [], ([[]], [[]])
    for start, count in chains:
        gate_cut = gate_pre[start : start + count].astype(jnp.float32)
        up_cut = up_pre[start : start + count].astype(jnp.float32)
        hidden.append((gate_cut * jax.nn.sigmoid(gate_cut) * up_cut).astype(jnp.bfloat16))
        for way, steps in enumerate(ways):
            steps[0].append(ring(hidden[-1].astype(wire), way))

    cot = spread_cotangent(grad_out, hidden, [steps[0][0] for steps in ways], [steps[0][1] for steps in ways])
    turn = hidden[0]
    for step in range(2, rows + 1):
        for steps in ways:
            steps.append([])
        for at, (first, _) in enumerate(chains):
            for way, steps in enumerate(ways):
                got = after(steps[-2][at], turn)
                turn = add_share(got, cot, down_t, way, step, first, tok_rows)
                steps[-1].append(ring(turn, way))
        late = turn

    weight_grad = weight_product(cot, jnp.concatenate(hidden), [steps[:-1] for steps in ways], norm_scale)

    own_share = jnp.dot(after(cot[:tok_rows], late), down_t, preferred_element_type=jnp.float32)
    own_share, gate_again, up_again = after((own_share, gate_pre, up_pre), turn)
    grads = None
    for at, (first, _) in enumerate(chains):
        grads = finish(gate_again, up_again, own_share, ways[0][-1][at], ways[1][-1][at], first, grads)
    return *grads, weight_grad


def solution(mesh):
    specs = (P("row", "col"),) * 4
    return jax.shard_map(
        per_device, mesh=mesh, in_specs=specs, out_specs=specs[:3], check_vma=False
    )
```

```python
import jax
import jax.numpy as jnp
from jax import lax
from jax.experimental import pallas as pl
from jax.experimental.pallas import tpu as pltpu
from jax.sharding import PartitionSpec as P


def after(value, first):
    return lax.optimization_barrier((value, first))[0]


def lay_strips(near, far, groups):
    chips = len(near)
    _, strip, width = near[0].shape

    def kernel(*refs):
        rows, row, col = lax.axis_size("row"), lax.axis_index("row"), lax.axis_index("col")
        out_ref = refs[-1]
        for at, ref in enumerate(refs[:-1]):
            core, chip = at // chips, at % chips
            lane = pl.multiple_of(((col & 1) ^ core) * width, width)
            for at_group, group in enumerate(groups):
                slot = lax.rem((row ^ group) + rows - row, rows) - groups[0]
                start = (slot * chips + (col // 2 ^ chip)) * strip
                out_ref[pl.ds(pl.multiple_of(start, strip), strip), pl.ds(lane, width)] = ref[at_group]

    return pl.pallas_call(
        kernel,
        out_shape=jax.ShapeDtypeStruct((len(groups) * chips * strip, 2 * width), near[0].dtype),
        in_specs=[pl.BlockSpec(memory_space=pltpu.VMEM)] * 2 * chips,
        out_specs=pl.BlockSpec(memory_space=pltpu.VMEM),
        compiler_params=pltpu.CompilerParams(vmem_limit_bytes=32 * 2**20),
        name="lay_strips",
    )(*near, *far)


def goes_ahead(way):
    return (lax.axis_index("col") & 1) == way


def ring(value, way):
    rows, cols = lax.axis_size("row"), lax.axis_size("col")
    pairs = []
    for row in range(rows):
        for col in range(cols):
            to = row + 1 if col & 1 == way else row - 1
            if 0 <= to < rows:
                pairs.append((row * cols + col, to * cols + col))
    return lax.ppermute(value, ("row", "col"), pairs)


def add_share(got, cot, down_t, way, step, first, tok_rows):
    span, width = got.shape
    tile = 512 if width % 512 == 0 else width

    def kernel(got_ref, cot_ref, down_ref, out_ref):
        rows, row, ahead = lax.axis_size("row"), lax.axis_index("row"), goes_ahead(way)
        is_sum = step > jnp.where(ahead, row + 1, rows - row)
        start = jnp.where(ahead, rows - step, step - 2) * tok_rows + first

        @pl.when(is_sum)
        def _():
            tokens = cot_ref[pl.ds(pl.multiple_of(start, 16), span), :]
            for at in range(0, width, tile):
                cut = slice(at, at + tile)
                share = jnp.dot(tokens, down_ref[:, cut], preferred_element_type=jnp.float32)
                out_ref[:, cut] = (got_ref[:, cut].astype(jnp.float32) + share).astype(out_ref.dtype)

        @pl.when(jnp.logical_not(is_sum))
        def _():
            out_ref[...] = got_ref[...]

    whole = pl.BlockSpec(memory_space=pltpu.VMEM)
    return pl.pallas_call(
        kernel,
        out_shape=jax.ShapeDtypeStruct(got.shape, got.dtype),
        in_specs=[whole] * 3,
        out_specs=whole,
        compiler_params=pltpu.CompilerParams(vmem_limit_bytes=32 * 2**20),
        cost_estimate=pl.CostEstimate(
            flops=2 * span * down_t.size, bytes_accessed=4 * span * width, transcendentals=0
        ),
        name="add_share",
    )(got, cot, down_t)


def weight_product(own_cot, cot, own, ways, scale):
    rows = len(ways[0]) + 1
    tok_rows, width = own.shape
    tile = 512 if width % 512 == 0 else width
    flat = [piece for steps in ways for pieces in steps for piece in pieces]

    def kernel(own_cot_ref, cot_ref, own_ref, *refs):
        ends, (out_ref, hidden_ref) = iter(refs[: len(flat)]), refs[len(flat) :]
        way_refs = [[[next(ends) for _ in pieces] for pieces in steps] for steps in ways]
        row = lax.axis_index("row")

        def place(pieces, start, cut):
            for piece in pieces:
                hidden_ref[start : start + piece.shape[0], :] = piece[:, cut].astype(hidden_ref.dtype)
                start += piece.shape[0]

        @pl.loop(0, width // tile)
        def _(at):
            cut = pl.ds(pl.multiple_of(at * tile, tile), tile)
            place([own_ref], 0, cut)
            for slot in range(1, rows):
                for way, refs_of in enumerate(way_refs):
                    ahead, from_next = goes_ahead(way), row + slot < rows
                    for here, step in (
                        (jnp.logical_and(from_next, jnp.logical_not(ahead)), slot),
                        (jnp.logical_and(jnp.logical_not(from_next), ahead), rows - slot),
                    ):
                        pieces = refs_of[step - 1]
                        pl.when(here)(lambda pieces=pieces, slot=slot: place(pieces, slot * tok_rows, cut))
            total = sum(
                lax.dot_general(
                    tokens[...], blocks, (((0,), (0,)), ((), ())), preferred_element_type=jnp.float32
                )
                for tokens, blocks in (
                    (own_cot_ref, hidden_ref[:tok_rows, :]),
                    (cot_ref, hidden_ref[tok_rows:, :]),
                )
            )
            out_ref[:, cut] = (total * scale).astype(out_ref.dtype)

    whole = pl.BlockSpec(memory_space=pltpu.VMEM)
    return pl.pallas_call(
        kernel,
        out_shape=jax.ShapeDtypeStruct((cot.shape[1], width), jnp.bfloat16),
        in_specs=[whole] * (3 + len(flat)),
        out_specs=whole,
        scratch_shapes=[pltpu.VMEM((rows * tok_rows, tile), jnp.bfloat16)],
        compiler_params=pltpu.CompilerParams(vmem_limit_bytes=32 * 2**20),
        cost_estimate=pl.CostEstimate(
            flops=2 * rows * own_cot.size * width, bytes_accessed=4 * rows * tok_rows * width, transcendentals=0
        ),
        name="weight_product",
    )(own_cot, cot, own, *flat)


def finish(gate_pre, up_pre, share, fore, back, start, grads):
    span, width = fore.shape
    tile = 512 if width % 512 == 0 else width
    old = () if grads is None else tuple(grads)

    def kernel(*refs):
        gate_ref, up_ref, share_ref, fore_ref, back_ref = refs[:5]
        outs, parts, sems = refs[5 + len(old) : 7 + len(old)], refs[-3:-1], refs[-1]
        here = slice(start, start + span)
        copies = []
        for at in range(0, width, tile):
            cut = slice(at, at + tile)
            grad = share_ref[here, cut] + fore_ref[:, cut].astype(jnp.float32) + back_ref[:, cut].astype(jnp.float32)
            gate = gate_ref[here, cut].astype(jnp.float32)
            sigmoid = jax.nn.sigmoid(gate)
            slope = sigmoid * (1.0 + gate * (1.0 - sigmoid))
            parts[0][:, cut] = (grad * up_ref[here, cut].astype(jnp.float32) * slope).astype(jnp.bfloat16)
            parts[1][:, cut] = (grad * (gate * sigmoid)).astype(jnp.bfloat16)
            for which, (part, out) in enumerate(zip(parts, outs)):
                copy = pltpu.make_async_copy(part.at[:, cut], out.at[here, cut], sems.at[which, at // tile])
                copy.start()
                copies.append(copy)
        for copy in copies:
            copy.wait()

    whole, anywhere = pl.BlockSpec(memory_space=pltpu.VMEM), pl.BlockSpec(memory_space=pl.ANY)
    return pl.pallas_call(
        kernel,
        out_shape=[jax.ShapeDtypeStruct(gate_pre.shape, jnp.bfloat16)] * 2,
        in_specs=[whole] * 5 + [anywhere] * len(old),
        out_specs=[anywhere] * 2,
        scratch_shapes=[pltpu.VMEM((span, width), jnp.bfloat16)] * 2
        + [pltpu.SemaphoreType.DMA((2, width // tile))],
        input_output_aliases={5 + at: at for at in range(len(old))},
        compiler_params=pltpu.CompilerParams(vmem_limit_bytes=32 * 2**20),
        cost_estimate=pl.CostEstimate(flops=20 * span * width, bytes_accessed=8 * span * width, transcendentals=span * width),
        name="finish",
    )(gate_pre, up_pre, share, fore, back, *old)


def swap(value, bits):
    return lax.ppermute(value, "col", [(at, at ^ bits) for at in range(lax.axis_size("col"))])


def spread_cotangent(grad_out, hidden, first, second):
    rows, cols = lax.axis_size("row"), lax.axis_size("col")
    row = lax.axis_index("row")
    tok_rows, width = grad_out.shape
    per_row = cols // rows
    if (rows, cols) != (4, 8):
        pairs = [
            (src * cols + per_row * dst + part, dst * cols + per_row * ((src - dst) % rows) + part)
            for src in range(rows)
            for dst in range(rows)
            for part in range(per_row)
        ]
        moved = lax.ppermute(grad_out, ("row", "col"), pairs)
        blocks = lax.all_gather(moved, "col", axis=0)
        blocks = blocks.reshape(rows, per_row, tok_rows, width)
        cot = blocks.transpose(0, 2, 1, 3).reshape(rows * tok_rows, per_row * width)
        return cot[tok_rows:], lambda stage, value, first: cot[:tok_rows]
    strip = tok_rows * 2 // cols
    chip = lax.axis_index("col") // 2

    def quarter(bits):
        piece = lax.dynamic_slice_in_dim(grad_out, (chip ^ bits) * strip, strip, 0)
        return swap(piece, 2 * bits) if bits else piece

    wide = after([quarter(bits) for bits in range(cols // 2)], hidden[0])

    def across(bits):
        piece = lax.dynamic_index_in_dim(jnp.stack(wide), chip ^ row ^ bits, 0, keepdims=False)
        return lax.ppermute(piece, "row", [(at, at ^ bits) for at in range(rows)]) if bits else piece

    tall = [across(bits) for bits in range(rows - 1, -1, -1)]
    own, tall = tall[-1], jnp.stack(tall[-2::-1])
    near = [tall, swap(tall, 2), swap(tall, 4), swap(tall, 6)]
    near[3] = after(near[3], first)
    far = [swap(block, 1) for block in near]
    far = after(far, second[0])

    own = own[None]

    def own_group(stage, value, first):
        if stage < 2:
            value = after(own if stage == 0 else value, first)
            return jnp.concatenate([value, swap(value, (2, 4)[stage])])
        near = after(value, first)
        far = swap(near, 1)
        return lay_strips(*([block[None] for block in blocks] for blocks in (near, far)), range(1))

    return lay_strips(near, far, range(1, rows)), own_group


def per_device(gate_pre, up_pre, down_t, grad_out):
    rows = lax.axis_size("row")
    tok_rows, width = gate_pre.shape
    norm_scale = (tok_rows * rows) ** (-0.5)
    wire = jnp.bfloat16 if rows <= 4 else jnp.float32
    lead = tok_rows * 8 // 16
    chains = ((0, lead), (lead, tok_rows - lead))

    hidden, ways = [], ([[]], [[]])
    for start, count in chains:
        gate_cut = gate_pre[start : start + count].astype(jnp.float32)
        up_cut = up_pre[start : start + count].astype(jnp.float32)
        hidden.append((gate_cut * jax.nn.sigmoid(gate_cut) * up_cut).astype(jnp.bfloat16))
        for way, steps in enumerate(ways):
            steps[0].append(ring(hidden[-1].astype(wire), way))

    cot, own_group = spread_cotangent(grad_out, hidden, [steps[0][0] for steps in ways], [steps[0][1] for steps in ways])
    turn = hidden[0]
    own_cot, stage = None, 0
    for step in range(2, rows + 1):
        for steps in ways:
            steps.append([])
        for at, (first, _) in enumerate(chains):
            for way, steps in enumerate(ways):
                got = after(steps[-2][at], turn)
                turn = add_share(got, cot, down_t, way, step, first, tok_rows)
                steps[-1].append(ring(turn, way))
                if (step, at, way) in ((2, 1, 1), (3, 0, 1), (3, 1, 1)):
                    own_cot, stage = own_group(stage, own_cot, turn), stage + 1
        late = turn

    weight_grad = weight_product(own_cot, cot, jnp.concatenate(hidden), [steps[:-1] for steps in ways], norm_scale)

    own_share = jnp.dot(after(own_cot, late), down_t, preferred_element_type=jnp.float32)
    own_share, gate_again, up_again = after((own_share, gate_pre, up_pre), turn)
    grads = None
    for at, (first, _) in enumerate(chains):
        grads = finish(gate_again, up_again, own_share, ways[0][-1][at], ways[1][-1][at], first, grads)
    return *grads, weight_grad


def solution(mesh):
    specs = (P("row", "col"),) * 4
    return jax.shard_map(
        per_device, mesh=mesh, in_specs=specs, out_specs=specs[:3], check_vma=False
    )
```

```python
import jax
import jax.numpy as jnp
from jax import lax
from jax.experimental import pallas as pl
from jax.experimental.pallas import tpu as pltpu
from jax.sharding import PartitionSpec as P


def after(value, first):
    return lax.optimization_barrier((value, first))[0]


def lay_strips(near, far, groups):
    chips = len(near)
    _, strip, width = near[0].shape

    def kernel(*refs):
        rows, row, col = lax.axis_size("row"), lax.axis_index("row"), lax.axis_index("col")
        out_ref = refs[-1]
        for at, ref in enumerate(refs[:-1]):
            core, chip = at // chips, at % chips
            lane = pl.multiple_of(((col & 1) ^ core) * width, width)
            for at_group, group in enumerate(groups):
                slot = lax.rem((row ^ group) + rows - row, rows) - groups[0]
                start = (slot * chips + (col // 2 ^ chip)) * strip
                out_ref[pl.ds(pl.multiple_of(start, strip), strip), pl.ds(lane, width)] = ref[at_group]

    return pl.pallas_call(
        kernel,
        out_shape=jax.ShapeDtypeStruct((len(groups) * chips * strip, 2 * width), near[0].dtype),
        in_specs=[pl.BlockSpec(memory_space=pltpu.VMEM)] * 2 * chips,
        out_specs=pl.BlockSpec(memory_space=pltpu.VMEM),
        compiler_params=pltpu.CompilerParams(vmem_limit_bytes=32 * 2**20),
        name="lay_strips",
    )(*near, *far)


def goes_ahead(way):
    return (lax.axis_index("col") & 1) == way


def ring(value, way):
    rows, cols = lax.axis_size("row"), lax.axis_size("col")
    pairs = []
    for row in range(rows):
        for col in range(cols):
            to = row + 1 if col & 1 == way else row - 1
            if 0 <= to < rows:
                pairs.append((row * cols + col, to * cols + col))
    return lax.ppermute(value, ("row", "col"), pairs)


def add_share(got, cot, down_t, way, step, first, tok_rows):
    span, width = got.shape
    tile = 512 if width % 512 == 0 else width

    def kernel(got_ref, cot_ref, down_ref, out_ref):
        rows, row, ahead = lax.axis_size("row"), lax.axis_index("row"), goes_ahead(way)
        is_sum = step > jnp.where(ahead, row + 1, rows - row)
        start = jnp.where(ahead, rows - step, step - 2) * tok_rows + first

        @pl.when(is_sum)
        def _():
            tokens = cot_ref[pl.ds(pl.multiple_of(start, 16), span), :]
            for at in range(0, width, tile):
                cut = slice(at, at + tile)
                share = jnp.dot(tokens, down_ref[:, cut], preferred_element_type=jnp.float32)
                out_ref[:, cut] = (got_ref[:, cut].astype(jnp.float32) + share).astype(out_ref.dtype)

        @pl.when(jnp.logical_not(is_sum))
        def _():
            out_ref[...] = got_ref[...]

    whole = pl.BlockSpec(memory_space=pltpu.VMEM)
    return pl.pallas_call(
        kernel,
        out_shape=jax.ShapeDtypeStruct(got.shape, got.dtype),
        in_specs=[whole] * 3,
        out_specs=whole,
        compiler_params=pltpu.CompilerParams(vmem_limit_bytes=32 * 2**20),
        cost_estimate=pl.CostEstimate(
            flops=2 * span * down_t.size, bytes_accessed=4 * span * width, transcendentals=0
        ),
        name="add_share",
    )(got, cot, down_t)


def weight_product(own_cot, cot, own, ways, scale):
    rows = len(ways[0]) + 1
    tok_rows, width = own.shape
    tile = 512 if width % 512 == 0 else width
    flat = [piece for steps in ways for pieces in steps for piece in pieces]

    def kernel(own_cot_ref, cot_ref, own_ref, *refs):
        ends, (out_ref, hidden_ref) = iter(refs[: len(flat)]), refs[len(flat) :]
        way_refs = [[[next(ends) for _ in pieces] for pieces in steps] for steps in ways]
        row = lax.axis_index("row")

        def place(pieces, start, cut):
            for piece in pieces:
                hidden_ref[start : start + piece.shape[0], :] = piece[:, cut].astype(hidden_ref.dtype)
                start += piece.shape[0]

        @pl.loop(0, width // tile)
        def _(at):
            cut = pl.ds(pl.multiple_of(at * tile, tile), tile)
            place([own_ref], 0, cut)
            for slot in range(1, rows):
                for way, refs_of in enumerate(way_refs):
                    ahead, from_next = goes_ahead(way), row + slot < rows
                    for here, step in (
                        (jnp.logical_and(from_next, jnp.logical_not(ahead)), slot),
                        (jnp.logical_and(jnp.logical_not(from_next), ahead), rows - slot),
                    ):
                        pieces = refs_of[step - 1]
                        pl.when(here)(lambda pieces=pieces, slot=slot: place(pieces, slot * tok_rows, cut))
            total = sum(
                lax.dot_general(
                    tokens[...], blocks, (((0,), (0,)), ((), ())), preferred_element_type=jnp.float32
                )
                for tokens, blocks in (
                    (own_cot_ref, hidden_ref[:tok_rows, :]),
                    (cot_ref, hidden_ref[tok_rows:, :]),
                )
            )
            out_ref[:, cut] = (total * scale).astype(out_ref.dtype)

    whole = pl.BlockSpec(memory_space=pltpu.VMEM)
    return pl.pallas_call(
        kernel,
        out_shape=jax.ShapeDtypeStruct((cot.shape[1], width), jnp.bfloat16),
        in_specs=[whole] * (3 + len(flat)),
        out_specs=whole,
        scratch_shapes=[pltpu.VMEM((rows * tok_rows, tile), jnp.bfloat16)],
        compiler_params=pltpu.CompilerParams(vmem_limit_bytes=32 * 2**20),
        cost_estimate=pl.CostEstimate(
            flops=2 * rows * own_cot.size * width, bytes_accessed=4 * rows * tok_rows * width, transcendentals=0
        ),
        name="weight_product",
    )(own_cot, cot, own, *flat)


def factors_of(gate_value, up_value):
    gate_value, up_value = gate_value.astype(jnp.float32), up_value.astype(jnp.float32)
    gate_sigmoid = jax.nn.sigmoid(gate_value)
    return up_value * (gate_sigmoid * (1.0 + gate_value * (1.0 - gate_sigmoid))), gate_value * gate_sigmoid


def finish(sources, ready, share, fore, back, start, grads):
    span, width = fore.shape
    tile = 512 if width % 512 == 0 else width
    old = () if grads is None else tuple(grads)

    def kernel(*refs):
        source_refs, (share_ref, fore_ref, back_ref) = refs[:2], refs[2:5]
        outs, parts, sems = refs[5 + len(old) : 7 + len(old)], refs[-3:-1], refs[-1]
        here = slice(start, start + span)
        copies = []
        for at in range(0, width, tile):
            cut = slice(at, at + tile)
            grad = share_ref[here, cut] + fore_ref[:, cut].astype(jnp.float32) + back_ref[:, cut].astype(jnp.float32)
            factors = [ref[:, cut] for ref in source_refs] if ready else factors_of(*(ref[here, cut] for ref in source_refs))
            for which, (factor, part, out) in enumerate(zip(factors, parts, outs)):
                part[:, cut] = (grad * factor).astype(jnp.bfloat16)
                copy = pltpu.make_async_copy(part.at[:, cut], out.at[here, cut], sems.at[which, at // tile])
                copy.start()
                copies.append(copy)
        for copy in copies:
            copy.wait()

    whole, anywhere = pl.BlockSpec(memory_space=pltpu.VMEM), pl.BlockSpec(memory_space=pl.ANY)
    return pl.pallas_call(
        kernel,
        out_shape=[jax.ShapeDtypeStruct(share.shape, jnp.bfloat16)] * 2,
        in_specs=[whole] * 5 + [anywhere] * len(old),
        out_specs=[anywhere] * 2,
        scratch_shapes=[pltpu.VMEM((span, width), jnp.bfloat16)] * 2
        + [pltpu.SemaphoreType.DMA((2, width // tile))],
        input_output_aliases={5 + at: at for at in range(len(old))},
        compiler_params=pltpu.CompilerParams(vmem_limit_bytes=32 * 2**20),
        cost_estimate=pl.CostEstimate(flops=20 * span * width, bytes_accessed=8 * span * width, transcendentals=span * width),
        name="finish",
    )(*sources, share, fore, back, *old)


def swap(value, bits):
    return lax.ppermute(value, "col", [(at, at ^ bits) for at in range(lax.axis_size("col"))])


def spread_cotangent(grad_out, hidden, first, second):
    rows, cols = lax.axis_size("row"), lax.axis_size("col")
    row = lax.axis_index("row")
    tok_rows, width = grad_out.shape
    per_row = cols // rows
    if (rows, cols) != (4, 8):
        pairs = [
            (src * cols + per_row * dst + part, dst * cols + per_row * ((src - dst) % rows) + part)
            for src in range(rows)
            for dst in range(rows)
            for part in range(per_row)
        ]
        moved = lax.ppermute(grad_out, ("row", "col"), pairs)
        blocks = lax.all_gather(moved, "col", axis=0)
        blocks = blocks.reshape(rows, per_row, tok_rows, width)
        cot = blocks.transpose(0, 2, 1, 3).reshape(rows * tok_rows, per_row * width)
        return cot[tok_rows:], lambda stage, value, first: cot[:tok_rows]
    strip = tok_rows * 2 // cols
    chip = lax.axis_index("col") // 2

    def quarter(bits):
        piece = lax.dynamic_slice_in_dim(grad_out, (chip ^ bits) * strip, strip, 0)
        return swap(piece, 2 * bits) if bits else piece

    wide = after([quarter(bits) for bits in range(cols // 2)], hidden[0])

    def across(bits):
        piece = lax.dynamic_index_in_dim(jnp.stack(wide), chip ^ row ^ bits, 0, keepdims=False)
        return lax.ppermute(piece, "row", [(at, at ^ bits) for at in range(rows)]) if bits else piece

    tall = [across(bits) for bits in range(rows - 1, -1, -1)]
    own, tall = tall[-1], jnp.stack(tall[-2::-1])
    near = [tall, swap(tall, 2), swap(tall, 4), swap(tall, 6)]
    near[0] = after(near[0], [first[0]])
    near[1] = after(near[1], [first[1]])
    far = [swap(block, 1) for block in near]
    far[3] = after(far[3], [second[0]])

    own = own[None]

    def own_group(stage, value, first):
        if stage < 2:
            value = after(own if stage == 0 else value, first)
            return jnp.concatenate([value, swap(value, (2, 4)[stage])])
        near = after(value, first)
        far = swap(near, 1)
        return lay_strips(*([block[None] for block in blocks] for blocks in (near, far)), range(1))

    return lay_strips(near, far, range(1, rows)), own_group


def per_device(gate_pre, up_pre, down_t, grad_out):
    rows = lax.axis_size("row")
    tok_rows, width = gate_pre.shape
    norm_scale = (tok_rows * rows) ** (-0.5)
    wire = jnp.bfloat16 if rows <= 4 else jnp.float32
    lead = tok_rows * 8 // 16
    chains = ((0, lead), (lead, tok_rows - lead))

    hidden, ways = [], ([[]], [[]])
    for start, count in chains:
        gate_cut = gate_pre[start : start + count].astype(jnp.float32)
        up_cut = up_pre[start : start + count].astype(jnp.float32)
        hidden.append((gate_cut * jax.nn.sigmoid(gate_cut) * up_cut).astype(jnp.bfloat16))
        for way, steps in enumerate(ways):
            steps[0].append(ring(hidden[-1].astype(wire), way))

    cot, own_group = spread_cotangent(grad_out, hidden, [steps[0][0] for steps in ways], [steps[0][1] for steps in ways])
    turn = hidden[0]
    own_cot, stage = None, 0
    for step in range(2, rows + 1):
        for steps in ways:
            steps.append([])
        for at, (first, _) in enumerate(chains):
            for way, steps in enumerate(ways):
                got = after(steps[-2][at], turn)
                turn = add_share(got, cot, down_t, way, step, first, tok_rows)
                steps[-1].append(ring(turn, way))
                if (step, at, way) in ((2, 1, 1), (3, 0, 1), (3, 1, 1)):
                    own_cot, stage = own_group(stage, own_cot, turn), stage + 1
        late = turn

    weight_grad = weight_product(own_cot, cot, jnp.concatenate(hidden), [steps[:-1] for steps in ways], norm_scale)

    own_share = jnp.dot(after(own_cot, late), down_t, preferred_element_type=jnp.float32)
    last, count = chains[-1]
    factors = factors_of(*(value[last : last + count] for value in after((gate_pre, up_pre), late)))
    own_share, gate_again, up_again = after((own_share, gate_pre, up_pre), turn)
    grads = None
    for at, (first, _) in enumerate(chains):
        ready = first == last
        sources = factors if ready else (gate_again, up_again)
        grads = finish(sources, ready, own_share, ways[0][-1][at], ways[1][-1][at], first, grads)
    return *grads, weight_grad


def solution(mesh):
    specs = (P("row", "col"),) * 4
    return jax.shard_map(
        per_device, mesh=mesh, in_specs=specs, out_specs=specs[:3], check_vma=False
    )
```

```python
import jax
import jax.numpy as jnp
from jax import lax
from jax.experimental import pallas as pl
from jax.experimental.pallas import tpu as pltpu
from jax.sharding import PartitionSpec as P


def after(value, first):
    return lax.optimization_barrier((value, first))[0]


def lay_strips(near, far, groups):
    chips = len(near)
    _, strip, width = near[0].shape

    def kernel(*refs):
        rows, row, col = lax.axis_size("row"), lax.axis_index("row"), lax.axis_index("col")
        out_ref = refs[-1]
        for at, ref in enumerate(refs[:-1]):
            core, chip = at // chips, at % chips
            lane = pl.multiple_of(((col & 1) ^ core) * width, width)
            for at_group, group in enumerate(groups):
                slot = lax.rem((row ^ group) + rows - row, rows) - groups[0]
                start = (slot * chips + (col // 2 ^ chip)) * strip
                out_ref[pl.ds(pl.multiple_of(start, strip), strip), pl.ds(lane, width)] = ref[at_group]

    return pl.pallas_call(
        kernel,
        out_shape=jax.ShapeDtypeStruct((len(groups) * chips * strip, 2 * width), near[0].dtype),
        in_specs=[pl.BlockSpec(memory_space=pltpu.VMEM)] * 2 * chips,
        out_specs=pl.BlockSpec(memory_space=pltpu.VMEM),
        compiler_params=pltpu.CompilerParams(vmem_limit_bytes=32 * 2**20),
        name="lay_strips",
    )(*near, *far)


def goes_ahead(way):
    return (lax.axis_index("col") & 1) == way


def ring(value, way):
    rows, cols = lax.axis_size("row"), lax.axis_size("col")
    pairs = []
    for row in range(rows):
        for col in range(cols):
            to = row + 1 if col & 1 == way else row - 1
            if 0 <= to < rows:
                pairs.append((row * cols + col, to * cols + col))
    return lax.ppermute(value, ("row", "col"), pairs)


def add_share(got, cot, down_t, way, step, first, tok_rows):
    span, width = got.shape
    tile = 512 if width % 512 == 0 else width

    def kernel(got_ref, cot_ref, down_ref, out_ref):
        rows, row, ahead = lax.axis_size("row"), lax.axis_index("row"), goes_ahead(way)
        is_sum = step > jnp.where(ahead, row + 1, rows - row)
        start = jnp.where(ahead, rows - step, step - 2) * tok_rows + first

        @pl.when(is_sum)
        def _():
            tokens = cot_ref[pl.ds(pl.multiple_of(start, 16), span), :]
            for at in range(0, width, tile):
                cut = slice(at, at + tile)
                share = jnp.dot(tokens, down_ref[:, cut], preferred_element_type=jnp.float32)
                out_ref[:, cut] = (got_ref[:, cut].astype(jnp.float32) + share).astype(out_ref.dtype)

        @pl.when(jnp.logical_not(is_sum))
        def _():
            out_ref[...] = got_ref[...]

    whole = pl.BlockSpec(memory_space=pltpu.VMEM)
    return pl.pallas_call(
        kernel,
        out_shape=jax.ShapeDtypeStruct(got.shape, got.dtype),
        in_specs=[whole] * 3,
        out_specs=whole,
        compiler_params=pltpu.CompilerParams(vmem_limit_bytes=32 * 2**20),
        cost_estimate=pl.CostEstimate(
            flops=2 * span * down_t.size, bytes_accessed=4 * span * width, transcendentals=0
        ),
        name="add_share",
    )(got, cot, down_t)


def weight_product(own_cot, cot, own, ways, scale):
    rows = len(ways[0]) + 1
    tok_rows, width = own.shape
    tile = 512 if width % 512 == 0 else width
    flat = [piece for steps in ways for pieces in steps for piece in pieces]

    def kernel(own_cot_ref, cot_ref, own_ref, *refs):
        ends, (out_ref, hidden_ref) = iter(refs[: len(flat)]), refs[len(flat) :]
        way_refs = [[[next(ends) for _ in pieces] for pieces in steps] for steps in ways]
        row = lax.axis_index("row")

        def place(pieces, start, cut):
            for piece in pieces:
                hidden_ref[start : start + piece.shape[0], :] = piece[:, cut].astype(hidden_ref.dtype)
                start += piece.shape[0]

        @pl.loop(0, width // tile)
        def _(at):
            cut = pl.ds(pl.multiple_of(at * tile, tile), tile)
            place([own_ref], 0, cut)
            for slot in range(1, rows):
                for way, refs_of in enumerate(way_refs):
                    ahead, from_next = goes_ahead(way), row + slot < rows
                    for here, step in (
                        (jnp.logical_and(from_next, jnp.logical_not(ahead)), slot),
                        (jnp.logical_and(jnp.logical_not(from_next), ahead), rows - slot),
                    ):
                        pieces = refs_of[step - 1]
                        pl.when(here)(lambda pieces=pieces, slot=slot: place(pieces, slot * tok_rows, cut))
            total = sum(
                lax.dot_general(
                    tokens[...], blocks, (((0,), (0,)), ((), ())), preferred_element_type=jnp.float32
                )
                for tokens, blocks in (
                    (own_cot_ref, hidden_ref[:tok_rows, :]),
                    (cot_ref, hidden_ref[tok_rows:, :]),
                )
            )
            out_ref[:, cut] = (total * scale).astype(out_ref.dtype)

    whole = pl.BlockSpec(memory_space=pltpu.VMEM)
    return pl.pallas_call(
        kernel,
        out_shape=jax.ShapeDtypeStruct((cot.shape[1], width), jnp.bfloat16),
        in_specs=[whole] * (3 + len(flat)),
        out_specs=whole,
        scratch_shapes=[pltpu.VMEM((rows * tok_rows, tile), jnp.bfloat16)],
        compiler_params=pltpu.CompilerParams(vmem_limit_bytes=32 * 2**20),
        cost_estimate=pl.CostEstimate(
            flops=2 * rows * own_cot.size * width, bytes_accessed=4 * rows * tok_rows * width, transcendentals=0
        ),
        name="weight_product",
    )(own_cot, cot, own, *flat)


def factors_of(gate_value, up_value):
    gate_value, up_value = gate_value.astype(jnp.float32), up_value.astype(jnp.float32)
    gate_sigmoid = jax.nn.sigmoid(gate_value)
    return up_value * (gate_sigmoid * (1.0 + gate_value * (1.0 - gate_sigmoid))), gate_value * gate_sigmoid


def finish(sources, ready, share, fore, back, start, grads):
    span, width = fore.shape
    tile = 512 if width % 512 == 0 else width
    old = () if grads is None else tuple(grads)

    def kernel(*refs):
        source_refs, (share_ref, fore_ref, back_ref) = refs[:2], refs[2:5]
        outs, parts, sems = refs[5 + len(old) : 7 + len(old)], refs[-3:-1], refs[-1]
        here = slice(start, start + span)
        copies = []
        for at in range(0, width, tile):
            cut = slice(at, at + tile)
            grad = share_ref[here, cut] + fore_ref[:, cut].astype(jnp.float32) + back_ref[:, cut].astype(jnp.float32)
            factors = [ref[:, cut] for ref in source_refs] if ready else factors_of(*(ref[here, cut] for ref in source_refs))
            for which, (factor, part, out) in enumerate(zip(factors, parts, outs)):
                part[:, cut] = (grad * factor).astype(jnp.bfloat16)
                copy = pltpu.make_async_copy(part.at[:, cut], out.at[here, cut], sems.at[which, at // tile])
                copy.start()
                copies.append(copy)
        for copy in copies:
            copy.wait()

    whole, anywhere = pl.BlockSpec(memory_space=pltpu.VMEM), pl.BlockSpec(memory_space=pl.ANY)
    return pl.pallas_call(
        kernel,
        out_shape=[jax.ShapeDtypeStruct(share.shape, jnp.bfloat16)] * 2,
        in_specs=[whole] * 5 + [anywhere] * len(old),
        out_specs=[anywhere] * 2,
        scratch_shapes=[pltpu.VMEM((span, width), jnp.bfloat16)] * 2
        + [pltpu.SemaphoreType.DMA((2, width // tile))],
        input_output_aliases={5 + at: at for at in range(len(old))},
        compiler_params=pltpu.CompilerParams(vmem_limit_bytes=32 * 2**20),
        cost_estimate=pl.CostEstimate(flops=20 * span * width, bytes_accessed=8 * span * width, transcendentals=span * width),
        name="finish",
    )(*sources, share, fore, back, *old)


def swap(value, bits):
    return lax.ppermute(value, "col", [(at, at ^ bits) for at in range(lax.axis_size("col"))])


def spread_cotangent(grad_out, hidden, first, second):
    rows, cols = lax.axis_size("row"), lax.axis_size("col")
    row = lax.axis_index("row")
    tok_rows, width = grad_out.shape
    per_row = cols // rows
    if (rows, cols) != (4, 8):
        pairs = [
            (src * cols + per_row * dst + part, dst * cols + per_row * ((src - dst) % rows) + part)
            for src in range(rows)
            for dst in range(rows)
            for part in range(per_row)
        ]
        moved = lax.ppermute(grad_out, ("row", "col"), pairs)
        blocks = lax.all_gather(moved, "col", axis=0)
        blocks = blocks.reshape(rows, per_row, tok_rows, width)
        cot = blocks.transpose(0, 2, 1, 3).reshape(rows * tok_rows, per_row * width)
        return cot[tok_rows:], lambda stage, value, first: cot[:tok_rows]
    strip = tok_rows * 2 // cols
    chip = lax.axis_index("col") // 2

    def quarter(bits):
        piece = lax.dynamic_slice_in_dim(grad_out, (chip ^ bits) * strip, strip, 0)
        return swap(piece, 2 * bits) if bits else piece

    wide = after([quarter(bits) for bits in range(cols // 2)], hidden[0])

    def across(bits):
        piece = lax.dynamic_index_in_dim(jnp.stack(wide), chip ^ row ^ bits, 0, keepdims=False)
        return lax.ppermute(piece, "row", [(at, at ^ bits) for at in range(rows)]) if bits else piece

    tall = [across(bits) for bits in range(rows - 1, -1, -1)]
    own, tall = tall[-1], jnp.stack(tall[-2::-1])
    near = [tall, swap(tall, 2), swap(tall, 4), swap(tall, 6)]
    near[3] = after(near[3], first)
    far = [swap(block, 1) for block in near]
    far = after(far, second[0])

    own = own[None]

    def own_group(stage, value, first):
        if stage < 2:
            value = after(own if stage == 0 else value, first)
            return jnp.concatenate([value, swap(value, (2, 4)[stage])])
        near = after(value, first)
        far = swap(near, 1)
        return lay_strips(*([block[None] for block in blocks] for blocks in (near, far)), range(1))

    return lay_strips(near, far, range(1, rows)), own_group


def per_device(gate_pre, up_pre, down_t, grad_out):
    rows = lax.axis_size("row")
    tok_rows, width = gate_pre.shape
    norm_scale = (tok_rows * rows) ** (-0.5)
    wire = jnp.bfloat16 if rows <= 4 else jnp.float32
    lead = tok_rows * 8 // 16
    chains = ((0, lead), (lead, tok_rows - lead))

    hidden, ways = [], ([[]], [[]])
    for start, count in chains:
        gate_cut = gate_pre[start : start + count].astype(jnp.float32)
        up_cut = up_pre[start : start + count].astype(jnp.float32)
        hidden.append((gate_cut * jax.nn.sigmoid(gate_cut) * up_cut).astype(jnp.bfloat16))
        for way, steps in enumerate(ways):
            steps[0].append(ring(hidden[-1].astype(wire), way))

    cot, own_group = spread_cotangent(grad_out, hidden, [steps[0][0] for steps in ways], [steps[0][1] for steps in ways])
    turn = hidden[0]
    own_cot, stage = None, 0
    for step in range(2, rows + 1):
        for steps in ways:
            steps.append([])
        for at, (first, _) in enumerate(chains):
            for way, steps in enumerate(ways):
                got = after(steps[-2][at], turn)
                turn = add_share(got, cot, down_t, way, step, first, tok_rows)
                steps[-1].append(ring(turn, way))
                if (step, at, way) in ((2, 1, 1), (3, 0, 1), (3, 1, 1)):
                    own_cot, stage = own_group(stage, own_cot, turn), stage + 1
        late = turn

    weight_grad = weight_product(own_cot, cot, jnp.concatenate(hidden), [steps[:-1] for steps in ways], norm_scale)

    own_share = jnp.dot(after(own_cot, late), down_t, preferred_element_type=jnp.float32)
    last, count = chains[-1]
    factors = factors_of(*(value[last : last + count] for value in after((gate_pre, up_pre), late)))
    own_share, gate_again, up_again = after((own_share, gate_pre, up_pre), turn)
    grads = None
    for at, (first, _) in enumerate(chains):
        ready = first == last
        sources = factors if ready else (gate_again, up_again)
        grads = finish(sources, ready, own_share, ways[0][-1][at], ways[1][-1][at], first, grads)
    return *grads, weight_grad


def solution(mesh):
    specs = (P("row", "col"),) * 4
    return jax.shard_map(
        per_device, mesh=mesh, in_specs=specs, out_specs=specs[:3], check_vma=False
    )
```

```python
import jax
import jax.numpy as jnp
from jax import lax
from jax.experimental import pallas as pl
from jax.experimental.pallas import tpu as pltpu
from jax.sharding import PartitionSpec as P


def after(value, first):
    return lax.optimization_barrier((value, first))[0]


def lay_strips(near, far, groups):
    chips = len(near)
    _, strip, width = near[0].shape

    def kernel(*refs):
        rows, row, col = lax.axis_size("row"), lax.axis_index("row"), lax.axis_index("col")
        out_ref = refs[-1]
        for at, ref in enumerate(refs[:-1]):
            core, chip = at // chips, at % chips
            lane = pl.multiple_of(((col & 1) ^ core) * width, width)
            for at_group, group in enumerate(groups):
                slot = lax.rem((row ^ group) + rows - row, rows) - groups[0]
                start = (slot * chips + (col // 2 ^ chip)) * strip
                out_ref[pl.ds(pl.multiple_of(start, strip), strip), pl.ds(lane, width)] = ref[at_group]

    return pl.pallas_call(
        kernel,
        out_shape=jax.ShapeDtypeStruct((len(groups) * chips * strip, 2 * width), near[0].dtype),
        in_specs=[pl.BlockSpec(memory_space=pltpu.VMEM)] * 2 * chips,
        out_specs=pl.BlockSpec(memory_space=pltpu.VMEM),
        compiler_params=pltpu.CompilerParams(vmem_limit_bytes=32 * 2**20),
        name="lay_strips",
    )(*near, *far)


def goes_ahead(way):
    return (lax.axis_index("col") & 1) == way


def ring(value, way):
    rows, cols = lax.axis_size("row"), lax.axis_size("col")
    pairs = []
    for row in range(rows):
        for col in range(cols):
            to = row + 1 if col & 1 == way else row - 1
            if 0 <= to < rows:
                pairs.append((row * cols + col, to * cols + col))
    return lax.ppermute(value, ("row", "col"), pairs)


def add_share(got, cot, down_t, way, step, first, tok_rows):
    span, width = got.shape
    tile = 512 if width % 512 == 0 else width

    def kernel(got_ref, cot_ref, down_ref, out_ref):
        rows, row, ahead = lax.axis_size("row"), lax.axis_index("row"), goes_ahead(way)
        is_sum = step > jnp.where(ahead, row + 1, rows - row)
        start = jnp.where(ahead, rows - step, step - 2) * tok_rows + first

        @pl.when(is_sum)
        def _():
            tokens = cot_ref[pl.ds(pl.multiple_of(start, 16), span), :]
            for at in range(0, width, tile):
                cut = slice(at, at + tile)
                share = jnp.dot(tokens, down_ref[:, cut], preferred_element_type=jnp.float32)
                out_ref[:, cut] = (got_ref[:, cut].astype(jnp.float32) + share).astype(out_ref.dtype)

        @pl.when(jnp.logical_not(is_sum))
        def _():
            out_ref[...] = got_ref[...]

    whole = pl.BlockSpec(memory_space=pltpu.VMEM)
    return pl.pallas_call(
        kernel,
        out_shape=jax.ShapeDtypeStruct(got.shape, got.dtype),
        in_specs=[whole] * 3,
        out_specs=whole,
        compiler_params=pltpu.CompilerParams(vmem_limit_bytes=32 * 2**20),
        cost_estimate=pl.CostEstimate(
            flops=2 * span * down_t.size, bytes_accessed=4 * span * width, transcendentals=0
        ),
        name="add_share",
    )(got, cot, down_t)


def weight_product(own_cot, cot, own, ways, scale):
    rows = len(ways[0]) + 1
    tok_rows, width = own.shape
    tile = 512 if width % 512 == 0 else width
    flat = [piece for steps in ways for pieces in steps for piece in pieces]

    def kernel(own_cot_ref, cot_ref, own_ref, *refs):
        ends, (out_ref, hidden_ref) = iter(refs[: len(flat)]), refs[len(flat) :]
        way_refs = [[[next(ends) for _ in pieces] for pieces in steps] for steps in ways]
        row = lax.axis_index("row")

        def place(pieces, start, cut):
            for piece in pieces:
                hidden_ref[start : start + piece.shape[0], :] = piece[:, cut].astype(hidden_ref.dtype)
                start += piece.shape[0]

        @pl.loop(0, width // tile)
        def _(at):
            cut = pl.ds(pl.multiple_of(at * tile, tile), tile)
            place([own_ref], 0, cut)
            for slot in range(1, rows):
                for way, refs_of in enumerate(way_refs):
                    ahead, from_next = goes_ahead(way), row + slot < rows
                    for here, step in (
                        (jnp.logical_and(from_next, jnp.logical_not(ahead)), slot),
                        (jnp.logical_and(jnp.logical_not(from_next), ahead), rows - slot),
                    ):
                        pieces = refs_of[step - 1]
                        pl.when(here)(lambda pieces=pieces, slot=slot: place(pieces, slot * tok_rows, cut))
            total = sum(
                lax.dot_general(
                    tokens[...], blocks, (((0,), (0,)), ((), ())), preferred_element_type=jnp.float32
                )
                for tokens, blocks in (
                    (own_cot_ref, hidden_ref[:tok_rows, :]),
                    (cot_ref, hidden_ref[tok_rows:, :]),
                )
            )
            out_ref[:, cut] = (total * scale).astype(out_ref.dtype)

    whole = pl.BlockSpec(memory_space=pltpu.VMEM)
    return pl.pallas_call(
        kernel,
        out_shape=jax.ShapeDtypeStruct((cot.shape[1], width), jnp.bfloat16),
        in_specs=[whole] * (3 + len(flat)),
        out_specs=whole,
        scratch_shapes=[pltpu.VMEM((rows * tok_rows, tile), jnp.bfloat16)],
        compiler_params=pltpu.CompilerParams(vmem_limit_bytes=32 * 2**20),
        cost_estimate=pl.CostEstimate(
            flops=2 * rows * own_cot.size * width, bytes_accessed=4 * rows * tok_rows * width, transcendentals=0
        ),
        name="weight_product",
    )(own_cot, cot, own, *flat)


def finish(gate_pre, up_pre, share, fore, back, start, grads):
    span, width = fore.shape
    tile = 512 if width % 512 == 0 else width
    old = () if grads is None else tuple(grads)

    def kernel(*refs):
        gate_ref, up_ref, share_ref, fore_ref, back_ref = refs[:5]
        outs, parts, sems = refs[5 + len(old) : 7 + len(old)], refs[-3:-1], refs[-1]
        here = slice(start, start + span)
        copies = []
        for at in range(0, width, tile):
            cut = slice(at, at + tile)
            grad = share_ref[here, cut] + fore_ref[:, cut].astype(jnp.float32) + back_ref[:, cut].astype(jnp.float32)
            gate = gate_ref[here, cut].astype(jnp.float32)
            sigmoid = jax.nn.sigmoid(gate)
            slope = sigmoid * (1.0 + gate * (1.0 - sigmoid))
            parts[0][:, cut] = (grad * up_ref[here, cut].astype(jnp.float32) * slope).astype(jnp.bfloat16)
            parts[1][:, cut] = (grad * (gate * sigmoid)).astype(jnp.bfloat16)
            for which, (part, out) in enumerate(zip(parts, outs)):
                copy = pltpu.make_async_copy(part.at[:, cut], out.at[here, cut], sems.at[which, at // tile])
                copy.start()
                copies.append(copy)
        for copy in copies:
            copy.wait()

    whole, anywhere = pl.BlockSpec(memory_space=pltpu.VMEM), pl.BlockSpec(memory_space=pl.ANY)
    return pl.pallas_call(
        kernel,
        out_shape=[jax.ShapeDtypeStruct(gate_pre.shape, jnp.bfloat16)] * 2,
        in_specs=[whole] * 5 + [anywhere] * len(old),
        out_specs=[anywhere] * 2,
        scratch_shapes=[pltpu.VMEM((span, width), jnp.bfloat16)] * 2
        + [pltpu.SemaphoreType.DMA((2, width // tile))],
        input_output_aliases={5 + at: at for at in range(len(old))},
        compiler_params=pltpu.CompilerParams(vmem_limit_bytes=32 * 2**20),
        cost_estimate=pl.CostEstimate(flops=20 * span * width, bytes_accessed=8 * span * width, transcendentals=span * width),
        name="finish",
    )(gate_pre, up_pre, share, fore, back, *old)


def swap(value, bits):
    return lax.ppermute(value, "col", [(at, at ^ bits) for at in range(lax.axis_size("col"))])


def spread_cotangent(grad_out, hidden, first, second):
    rows, cols = lax.axis_size("row"), lax.axis_size("col")
    row = lax.axis_index("row")
    tok_rows, width = grad_out.shape
    per_row = cols // rows
    if (rows, cols) != (4, 8):
        pairs = [
            (src * cols + per_row * dst + part, dst * cols + per_row * ((src - dst) % rows) + part)
            for src in range(rows)
            for dst in range(rows)
            for part in range(per_row)
        ]
        moved = lax.ppermute(grad_out, ("row", "col"), pairs)
        blocks = lax.all_gather(moved, "col", axis=0)
        blocks = blocks.reshape(rows, per_row, tok_rows, width)
        cot = blocks.transpose(0, 2, 1, 3).reshape(rows * tok_rows, per_row * width)
        return cot[tok_rows:], lambda stage, value, first: cot[:tok_rows]
    strip = tok_rows * 2 // cols
    chip = lax.axis_index("col") // 2

    def quarter(bits):
        piece = lax.dynamic_slice_in_dim(grad_out, (chip ^ bits) * strip, strip, 0)
        return swap(piece, 2 * bits) if bits else piece

    wide = after([quarter(bits) for bits in range(cols // 2)], hidden[0])

    def across(bits):
        piece = lax.dynamic_index_in_dim(jnp.stack(wide), chip ^ row ^ bits, 0, keepdims=False)
        return lax.ppermute(piece, "row", [(at, at ^ bits) for at in range(rows)]) if bits else piece

    tall = [across(bits) for bits in range(rows - 1, -1, -1)]
    own, tall = tall[-1], jnp.stack(tall[-2::-1])
    near = [tall, swap(tall, 2), swap(tall, 4), swap(tall, 6)]
    near[3] = after(near[3], first)
    far = [swap(block, 1) for block in near]
    far = after(far, second[0])

    own = own[None]

    def own_group(stage, value, first):
        if stage < 2:
            value = after(own if stage == 0 else value, first)
            return jnp.concatenate([value, swap(value, (2, 4)[stage])])
        near = after(value, first)
        far = swap(near, 1)
        return lay_strips(*([block[None] for block in blocks] for blocks in (near, far)), range(1))

    return lay_strips(near, far, range(1, rows)), own_group


def per_device(gate_pre, up_pre, down_t, grad_out):
    rows = lax.axis_size("row")
    tok_rows, width = gate_pre.shape
    norm_scale = (tok_rows * rows) ** (-0.5)
    wire = jnp.bfloat16 if rows <= 4 else jnp.float32
    lead = tok_rows * 8 // 16
    chains = ((0, lead), (lead, tok_rows - lead))

    hidden, ways = [], ([[]], [[]])
    for start, count in chains:
        gate_cut = gate_pre[start : start + count].astype(jnp.float32)
        up_cut = up_pre[start : start + count].astype(jnp.float32)
        hidden.append((gate_cut * jax.nn.sigmoid(gate_cut) * up_cut).astype(jnp.bfloat16))
        for way, steps in enumerate(ways):
            steps[0].append(ring(hidden[-1].astype(wire), way))

    cot, own_group = spread_cotangent(grad_out, hidden, [steps[0][0] for steps in ways], [steps[0][1] for steps in ways])
    turn = hidden[0]
    own_cot, stage = None, 0
    for step in range(2, rows + 1):
        for steps in ways:
            steps.append([])
        for at, (first, _) in enumerate(chains):
            for way, steps in enumerate(ways):
                got = after(steps[-2][at], turn)
                turn = add_share(got, cot, down_t, way, step, first, tok_rows)
                steps[-1].append(ring(turn, way))
                if (step, at, way) in ((3, 0, 0), (3, 1, 0), (4, 0, 0)):
                    own_cot, stage = own_group(stage, own_cot, turn), stage + 1
        late = turn

    weight_grad = weight_product(own_cot, cot, jnp.concatenate(hidden), [steps[:-1] for steps in ways], norm_scale)

    own_share = jnp.dot(after(own_cot, late), down_t, preferred_element_type=jnp.float32)
    own_share, gate_again, up_again = after((own_share, gate_pre, up_pre), turn)
    grads = None
    for at, (first, _) in enumerate(chains):
        grads = finish(gate_again, up_again, own_share, ways[0][-1][at], ways[1][-1][at], first, grads)
    return *grads, weight_grad


def solution(mesh):
    specs = (P("row", "col"),) * 4
    return jax.shard_map(
        per_device, mesh=mesh, in_specs=specs, out_specs=specs[:3], check_vma=False
    )
```

```python
import jax
import jax.numpy as jnp
from jax import lax
from jax.experimental import pallas as pl
from jax.experimental.pallas import tpu as pltpu
from jax.sharding import PartitionSpec as P


def after(value, first):
    return lax.optimization_barrier((value, first))[0]


def lay_strips(near, far, groups):
    chips = len(near)
    _, strip, width = near[0].shape

    def kernel(*refs):
        rows, row, col = lax.axis_size("row"), lax.axis_index("row"), lax.axis_index("col")
        out_ref = refs[-1]
        for at, ref in enumerate(refs[:-1]):
            core, chip = at // chips, at % chips
            lane = pl.multiple_of(((col & 1) ^ core) * width, width)
            for at_group, group in enumerate(groups):
                slot = lax.rem((row ^ group) + rows - row, rows) - groups[0]
                start = (slot * chips + (col // 2 ^ chip)) * strip
                out_ref[pl.ds(pl.multiple_of(start, strip), strip), pl.ds(lane, width)] = ref[at_group]

    return pl.pallas_call(
        kernel,
        out_shape=jax.ShapeDtypeStruct((len(groups) * chips * strip, 2 * width), near[0].dtype),
        in_specs=[pl.BlockSpec(memory_space=pltpu.VMEM)] * 2 * chips,
        out_specs=pl.BlockSpec(memory_space=pltpu.VMEM),
        compiler_params=pltpu.CompilerParams(vmem_limit_bytes=32 * 2**20),
        name="lay_strips",
    )(*near, *far)


def goes_ahead(way):
    return (lax.axis_index("col") & 1) == way


def ring(value, way):
    rows, cols = lax.axis_size("row"), lax.axis_size("col")
    pairs = []
    for row in range(rows):
        for col in range(cols):
            to = row + 1 if col & 1 == way else row - 1
            if 0 <= to < rows:
                pairs.append((row * cols + col, to * cols + col))
    return lax.ppermute(value, ("row", "col"), pairs)


def add_share(got, cot, down_t, way, step, first, tok_rows):
    span, width = got.shape
    tile = 512 if width % 512 == 0 else width

    def kernel(got_ref, cot_ref, down_ref, out_ref):
        rows, row, ahead = lax.axis_size("row"), lax.axis_index("row"), goes_ahead(way)
        is_sum = step > jnp.where(ahead, row + 1, rows - row)
        start = jnp.where(ahead, rows - step, step - 2) * tok_rows + first

        @pl.when(is_sum)
        def _():
            tokens = cot_ref[pl.ds(pl.multiple_of(start, 16), span), :]
            for at in range(0, width, tile):
                cut = slice(at, at + tile)
                share = jnp.dot(tokens, down_ref[:, cut], preferred_element_type=jnp.float32)
                out_ref[:, cut] = (got_ref[:, cut].astype(jnp.float32) + share).astype(out_ref.dtype)

        @pl.when(jnp.logical_not(is_sum))
        def _():
            out_ref[...] = got_ref[...]

    whole = pl.BlockSpec(memory_space=pltpu.VMEM)
    return pl.pallas_call(
        kernel,
        out_shape=jax.ShapeDtypeStruct(got.shape, got.dtype),
        in_specs=[whole] * 3,
        out_specs=whole,
        compiler_params=pltpu.CompilerParams(vmem_limit_bytes=32 * 2**20),
        cost_estimate=pl.CostEstimate(
            flops=2 * span * down_t.size, bytes_accessed=4 * span * width, transcendentals=0
        ),
        name="add_share",
    )(got, cot, down_t)


def weight_product(own_cot, cot, own, ways, scale):
    rows = len(ways[0]) + 1
    tok_rows, width = own.shape
    tile = 512 if width % 512 == 0 else width
    flat = [piece for steps in ways for pieces in steps for piece in pieces]

    def kernel(own_cot_ref, cot_ref, own_ref, *refs):
        ends, (out_ref, hidden_ref) = iter(refs[: len(flat)]), refs[len(flat) :]
        way_refs = [[[next(ends) for _ in pieces] for pieces in steps] for steps in ways]
        row = lax.axis_index("row")

        def place(pieces, start, cut):
            for piece in pieces:
                hidden_ref[start : start + piece.shape[0], :] = piece[:, cut].astype(hidden_ref.dtype)
                start += piece.shape[0]

        @pl.loop(0, width // tile)
        def _(at):
            cut = pl.ds(pl.multiple_of(at * tile, tile), tile)
            place([own_ref], 0, cut)
            for slot in range(1, rows):
                for way, refs_of in enumerate(way_refs):
                    ahead, from_next = goes_ahead(way), row + slot < rows
                    for here, step in (
                        (jnp.logical_and(from_next, jnp.logical_not(ahead)), slot),
                        (jnp.logical_and(jnp.logical_not(from_next), ahead), rows - slot),
                    ):
                        pieces = refs_of[step - 1]
                        pl.when(here)(lambda pieces=pieces, slot=slot: place(pieces, slot * tok_rows, cut))
            total = sum(
                lax.dot_general(
                    tokens[...], blocks, (((0,), (0,)), ((), ())), preferred_element_type=jnp.float32
                )
                for tokens, blocks in (
                    (own_cot_ref, hidden_ref[:tok_rows, :]),
                    (cot_ref, hidden_ref[tok_rows:, :]),
                )
            )
            out_ref[:, cut] = (total * scale).astype(out_ref.dtype)

    whole = pl.BlockSpec(memory_space=pltpu.VMEM)
    return pl.pallas_call(
        kernel,
        out_shape=jax.ShapeDtypeStruct((cot.shape[1], width), jnp.bfloat16),
        in_specs=[whole] * (3 + len(flat)),
        out_specs=whole,
        scratch_shapes=[pltpu.VMEM((rows * tok_rows, tile), jnp.bfloat16)],
        compiler_params=pltpu.CompilerParams(vmem_limit_bytes=32 * 2**20),
        cost_estimate=pl.CostEstimate(
            flops=2 * rows * own_cot.size * width, bytes_accessed=4 * rows * tok_rows * width, transcendentals=0
        ),
        name="weight_product",
    )(own_cot, cot, own, *flat)


def finish(gate_pre, up_pre, share, fore, back, start, grads):
    span, width = fore.shape
    tile = 1024 if width % 1024 == 0 else width
    old = () if grads is None else tuple(grads)

    def kernel(*refs):
        gate_ref, up_ref, share_ref, fore_ref, back_ref = refs[:5]
        outs, parts, sems = refs[5 + len(old) : 7 + len(old)], refs[-3:-1], refs[-1]
        here = slice(start, start + span)
        copies = []
        for at in range(0, width, tile):
            cut = slice(at, at + tile)
            grad = share_ref[here, cut] + fore_ref[:, cut].astype(jnp.float32) + back_ref[:, cut].astype(jnp.float32)
            gate = gate_ref[here, cut].astype(jnp.float32)
            sigmoid = jax.nn.sigmoid(gate)
            slope = sigmoid * (1.0 + gate * (1.0 - sigmoid))
            parts[0][:, cut] = (grad * up_ref[here, cut].astype(jnp.float32) * slope).astype(jnp.bfloat16)
            parts[1][:, cut] = (grad * (gate * sigmoid)).astype(jnp.bfloat16)
            for which, (part, out) in enumerate(zip(parts, outs)):
                copy = pltpu.make_async_copy(part.at[:, cut], out.at[here, cut], sems.at[which, at // tile])
                copy.start()
                copies.append(copy)
        for copy in copies:
            copy.wait()

    whole, anywhere = pl.BlockSpec(memory_space=pltpu.VMEM), pl.BlockSpec(memory_space=pl.ANY)
    return pl.pallas_call(
        kernel,
        out_shape=[jax.ShapeDtypeStruct(gate_pre.shape, jnp.bfloat16)] * 2,
        in_specs=[whole] * 5 + [anywhere] * len(old),
        out_specs=[anywhere] * 2,
        scratch_shapes=[pltpu.VMEM((span, width), jnp.bfloat16)] * 2
        + [pltpu.SemaphoreType.DMA((2, width // tile))],
        input_output_aliases={5 + at: at for at in range(len(old))},
        compiler_params=pltpu.CompilerParams(vmem_limit_bytes=32 * 2**20),
        cost_estimate=pl.CostEstimate(flops=20 * span * width, bytes_accessed=8 * span * width, transcendentals=span * width),
        name="finish",
    )(gate_pre, up_pre, share, fore, back, *old)


def swap(value, bits):
    return lax.ppermute(value, "col", [(at, at ^ bits) for at in range(lax.axis_size("col"))])


def spread_cotangent(grad_out, hidden, first, second):
    rows, cols = lax.axis_size("row"), lax.axis_size("col")
    row = lax.axis_index("row")
    tok_rows, width = grad_out.shape
    per_row = cols // rows
    if (rows, cols) != (4, 8):
        pairs = [
            (src * cols + per_row * dst + part, dst * cols + per_row * ((src - dst) % rows) + part)
            for src in range(rows)
            for dst in range(rows)
            for part in range(per_row)
        ]
        moved = lax.ppermute(grad_out, ("row", "col"), pairs)
        blocks = lax.all_gather(moved, "col", axis=0)
        blocks = blocks.reshape(rows, per_row, tok_rows, width)
        cot = blocks.transpose(0, 2, 1, 3).reshape(rows * tok_rows, per_row * width)
        return cot[tok_rows:], lambda stage, value, first: cot[:tok_rows]
    strip = tok_rows * 2 // cols
    chip = lax.axis_index("col") // 2

    def quarter(bits):
        piece = lax.dynamic_slice_in_dim(grad_out, (chip ^ bits) * strip, strip, 0)
        return swap(piece, 2 * bits) if bits else piece

    wide = after([quarter(bits) for bits in range(cols // 2)], hidden[0])

    def across(bits):
        piece = lax.dynamic_index_in_dim(jnp.stack(wide), chip ^ row ^ bits, 0, keepdims=False)
        return lax.ppermute(piece, "row", [(at, at ^ bits) for at in range(rows)]) if bits else piece

    tall = [across(bits) for bits in range(rows - 1, -1, -1)]
    own, tall = tall[-1], jnp.stack(tall[-2::-1])
    near = [tall, swap(tall, 2), swap(tall, 4), swap(tall, 6)]
    near[3] = after(near[3], first)
    far = [swap(block, 1) for block in near]
    far = after(far, second[0])

    own = own[None]

    def own_group(stage, value, first):
        if stage < 2:
            value = after(own if stage == 0 else value, first)
            return jnp.concatenate([value, swap(value, (2, 4)[stage])])
        near = after(value, first)
        far = swap(near, 1)
        return lay_strips(*([block[None] for block in blocks] for blocks in (near, far)), range(1))

    return lay_strips(near, far, range(1, rows)), own_group


def per_device(gate_pre, up_pre, down_t, grad_out):
    rows = lax.axis_size("row")
    tok_rows, width = gate_pre.shape
    norm_scale = (tok_rows * rows) ** (-0.5)
    wire = jnp.bfloat16 if rows <= 4 else jnp.float32
    lead = tok_rows * 8 // 16
    chains = ((0, lead), (lead, tok_rows - lead))

    hidden, ways = [], ([[]], [[]])
    for start, count in chains:
        gate_cut = gate_pre[start : start + count].astype(jnp.float32)
        up_cut = up_pre[start : start + count].astype(jnp.float32)
        hidden.append((gate_cut * jax.nn.sigmoid(gate_cut) * up_cut).astype(jnp.bfloat16))
        for way, steps in enumerate(ways):
            steps[0].append(ring(hidden[-1].astype(wire), way))

    cot, own_group = spread_cotangent(grad_out, hidden, [steps[0][0] for steps in ways], [steps[0][1] for steps in ways])
    turn = hidden[0]
    own_cot, stage = None, 0
    for step in range(2, rows + 1):
        for steps in ways:
            steps.append([])
        for at, (first, _) in enumerate(chains):
            for way, steps in enumerate(ways):
                got = after(steps[-2][at], turn)
                turn = add_share(got, cot, down_t, way, step, first, tok_rows)
                steps[-1].append(ring(turn, way))
                if (step, at, way) in ((2, 1, 1), (3, 0, 1), (3, 1, 1)):
                    own_cot, stage = own_group(stage, own_cot, turn), stage + 1
        late = turn

    weight_grad = weight_product(own_cot, cot, jnp.concatenate(hidden), [steps[:-1] for steps in ways], norm_scale)

    own_share = jnp.dot(after(own_cot, late), down_t, preferred_element_type=jnp.float32)
    own_share, gate_again, up_again = after((own_share, gate_pre, up_pre), turn)
    grads = None
    for at, (first, _) in enumerate(chains):
        grads = finish(gate_again, up_again, own_share, ways[0][-1][at], ways[1][-1][at], first, grads)
    return *grads, weight_grad


def solution(mesh):
    specs = (P("row", "col"),) * 4
    return jax.shard_map(
        per_device, mesh=mesh, in_specs=specs, out_specs=specs[:3], check_vma=False
    )
```
